32 devices in a mesh: seq: 16 (over z, x, core), dp: 2 (over y).
Axes of the slice: x: 2, y: 2, z: 4, core: 2. Of those that a mesh axis runs over, the one named last changes fastest.
Arguments:
- features: bfloat16 [2, 4096, 2048], P('dp', 'seq'), may hold values from -6 to 6
- queries: bfloat16 [2, 4096, 1024], P('dp', 'seq'), may hold values from -136 to 136
- kv_weight: bfloat16 [2048, 2048], P('dp'), may hold values from -0.125 to 0.125
- upstream: bfloat16 [2, 4096, 1024], P('dp', 'seq'), may hold values from -6 to 6
Outputs:
- attended: bfloat16 [2, 4096, 1024], P('dp', 'seq')
- query_grad: bfloat16 [2, 4096, 1024], P('dp', 'seq')
- feature_grad: bfloat16 [2, 4096, 2048], P('dp', 'seq')
- weight_grad: float32 [2048, 2048], P(('dp', 'seq'))
The draws below stay inside these ranges and needn't reach their ends.
All inputs are finite; a program needn't handle non-finite values.
Results may differ from the reference program's by a relative error of at most 0.013.
The reference program's roundings to bfloat16 on the way (of `own_kv`, `weights`, `dscore` and `kv_grad`) count: a program that leaves them out, or rounds other values in their place, can miss the bound.
Values may be sent and summed in bfloat16 or wider, within the bound.
No kernel may reach another device: no remote copies, remote signals or barrier semaphores. Data moves between devices by JAX's collectives and lax.ppermute only.
A program may use at most 128 MiB of HBM per device.

```python
import math
import jax
import jax.numpy as jnp
from jax import lax

D = 2048
HEADS = 8
HEAD_DIM = 128
WINDOW = 2048
TOK_DEV = 256
HW = 1024
TOKENS = 4096
SAMPLES = 2
N_SEQ = 16


def draw_queries(key, part):
    value_key = jax.random.fold_in(key, 21)
    shape = (SAMPLES, TOKENS, HEADS * HEAD_DIM)
    return jnp.clip(jax.random.normal(value_key, shape, jnp.float32), -5.0, 5.0).astype(jnp.bfloat16)


def draw_upstream(key, part):
    value_key = jax.random.fold_in(key, 31)
    shape = (SAMPLES, TOKENS, HEADS * HEAD_DIM)
    return jnp.clip(jax.random.normal(value_key, shape, jnp.float32), -6.0, 6.0).astype(jnp.bfloat16)


def spiked(entries, stream_key, source, target, parts, factor):
    owner, partner = [(jnp.arange(entries.shape[dim]) // (entries.shape[dim] // parts)).reshape([-1 if axis == dim else 1 for axis in range(entries.ndim)]) for dim in (source, target)]
    chosen = jax.random.permutation(stream_key, parts)[partner]
    strong = (owner == chosen) | (owner == (partner + parts // 2) % parts)
    return jnp.where(strong, factor * entries, entries)


def block_levels(stream_key, extent, pieces, least, high):
    loudness, own = 1.0, jax.random.fold_in(stream_key, 6)
    for position, shards_of in pieces:
        draws = jnp.exp(jax.random.uniform(jax.random.fold_in(own, position), (shards_of,), jnp.float32, least / len(pieces), high / len(pieces)))
        loudness = loudness * jnp.repeat(draws, extent[position] // shards_of).reshape([-1 if axis == position else 1 for axis in range(len(extent))])
    return loudness


def noise(stream_key, extent, deviation, reach, shards=(), kind=jnp.bfloat16):
    result = deviation * jax.random.normal(stream_key, extent, jnp.float32)
    if shards:
        result = result * block_levels(stream_key, extent, shards, -0.22, 0.18)
    return jnp.clip(result, -reach, reach).astype(kind)


def bell_draw_with(own_key, dims, width, bound, split, heavy, kind=jnp.bfloat16):
    entries = width * jax.random.normal(own_key, dims, jnp.float32)
    if split:
        entries = entries * block_levels(own_key, dims, split, -0.22, 0.18)
    return jnp.clip(spiked(entries, jax.random.fold_in(own_key, 3), *heavy), -bound, bound).astype(kind)


def setup_inputs(seed: int = 0) -> dict:
    streams_of = jax.random.split(jax.random.key(seed), 5)
    return {
        "features": bell_draw_with(streams_of[0], (SAMPLES, TOKENS, D), 1.0, 6.0, ((0, 2), (1, 16)), (1, 2, 16, 2.0)),
        "queries": draw_queries(jax.random.fold_in(streams_of[4], 71), 0),
        "kv_weight": noise(streams_of[2], (D, 2 * HW), D ** -0.5, 0.125, ((0, 2),)),
        "upstream": draw_upstream(jax.random.fold_in(streams_of[4], 71), 0),
    }


def attend_block(query_rows, upstream_rows, window_kv, block_index):
    span = WINDOW // TOK_DEV
    key_count = (span + 1) * TOK_DEV
    head_width = HEADS * HEAD_DIM
    score_scale = 1.0 / math.sqrt(HEAD_DIM)
    query_heads = query_rows.astype(jnp.float32).reshape(TOK_DEV, HEADS, HEAD_DIM)
    grad_heads = upstream_rows.astype(jnp.float32).reshape(TOK_DEV, HEADS, HEAD_DIM)
    key_heads = window_kv[:, :head_width].astype(jnp.float32).reshape(key_count, HEADS, HEAD_DIM)
    value_heads = window_kv[:, head_width:].astype(jnp.float32).reshape(key_count, HEADS, HEAD_DIM)
    query_pos = lax.broadcasted_iota(jnp.int32, (TOK_DEV, key_count), 0)
    key_pos = lax.broadcasted_iota(jnp.int32, (TOK_DEV, key_count), 1) - span * TOK_DEV
    first_pos = block_index.astype(jnp.int32) * TOK_DEV
    allowed = (key_pos <= query_pos) & (key_pos > query_pos - WINDOW) & (first_pos + key_pos >= 0)
    scores = jnp.einsum('ihd,jhd->hij', query_heads, key_heads) * score_scale
    scores = jnp.where(allowed[None], scores, -1e+30)
    row_max = lax.optimization_barrier(jnp.max(scores, axis=-1, keepdims=True))
    exp_scores = jnp.exp(scores - row_max)
    probability = exp_scores / lax.optimization_barrier(jnp.sum(exp_scores, axis=-1, keepdims=True))
    weights = probability.astype(jnp.bfloat16)
    weights_wide = lax.optimization_barrier(weights).astype(jnp.float32)
    attended = jnp.einsum('hij,jhd->ihd', weights_wide, value_heads).astype(jnp.bfloat16)
    dprob = jnp.einsum('ihd,jhd->hij', grad_heads, value_heads)
    centred = dprob - lax.optimization_barrier(jnp.sum(probability * dprob, axis=-1, keepdims=True))
    dscore = lax.optimization_barrier((probability * centred * score_scale).astype(jnp.bfloat16)).astype(jnp.float32)
    query_grad = jnp.einsum('hij,jhd->ihd', dscore, key_heads).astype(jnp.bfloat16)
    key_grad = jnp.einsum('hij,ihd->jhd', dscore, query_heads)
    value_grad = jnp.einsum('hij,ihd->jhd', weights_wide, grad_heads)
    kv_grad_all = jnp.concatenate([key_grad.reshape(key_count, head_width), value_grad.reshape(key_count, head_width)], axis=1)
    return (attended.reshape(TOK_DEV, head_width), query_grad.reshape(TOK_DEV, head_width), kv_grad_all)

def one_sample(item):
    own_kv, query_rows, upstream_rows = item
    span = WINDOW // TOK_DEV
    head_width = HEADS * HEAD_DIM
    padded = jnp.concatenate([jnp.zeros((span, TOK_DEV, 2 * head_width), jnp.bfloat16), own_kv], axis=0)
    zero_index = jnp.zeros((), jnp.int32)

    def visit(pending, inputs):
        query_block, upstream_block, block_index = inputs
        window_kv = lax.dynamic_slice(padded, (block_index.astype(jnp.int32), zero_index, zero_index), (span + 1, TOK_DEV, 2 * head_width))
        window_kv = window_kv.reshape((span + 1) * TOK_DEV, 2 * head_width)
        attended, query_grad, kv_grad_all = attend_block(query_block, upstream_block, window_kv, block_index)
        kv_grad_all = kv_grad_all.reshape(span + 1, TOK_DEV, 2 * head_width)
        own_total = kv_grad_all[span] + pending[0]
        remote = lax.optimization_barrier(kv_grad_all[:span].astype(jnp.bfloat16)).astype(jnp.float32)[::-1]
        shifted = jnp.concatenate([pending[1:], jnp.zeros((1, TOK_DEV, 2 * head_width), jnp.float32)], axis=0)
        return (shifted + remote, (attended, query_grad, own_total.astype(jnp.bfloat16)))
    start = jnp.zeros((span, TOK_DEV, 2 * head_width), jnp.float32)
    block_ids = jnp.arange(N_SEQ, dtype=jnp.int32)
    final, outputs = lax.scan(visit, start, (query_rows, upstream_rows, block_ids), reverse=True)
    return outputs

def reference(features, queries, kv_weight, upstream):
    head_width = HEADS * HEAD_DIM
    flat = features.reshape(SAMPLES * TOKENS, D)
    own_kv = jnp.dot(flat, kv_weight, preferred_element_type=jnp.float32).astype(jnp.bfloat16)
    own_kv = own_kv.reshape(SAMPLES, N_SEQ, TOK_DEV, 2 * head_width)
    query_rows = queries.reshape(SAMPLES, N_SEQ, TOK_DEV, head_width)
    upstream_rows = upstream.reshape(SAMPLES, N_SEQ, TOK_DEV, head_width)
    attended, query_grad, kv_grad = lax.map(one_sample, (own_kv, query_rows, upstream_rows))
    kv_grad = kv_grad.reshape(SAMPLES * TOKENS, 2 * head_width)
    feature_grad = lax.dot_general(kv_grad, kv_weight, (((1,), (1,)), ((), ())), preferred_element_type=jnp.float32)
    feature_grad = feature_grad.astype(jnp.bfloat16).reshape(SAMPLES, TOKENS, D)
    weight_grad = lax.dot_general(flat, kv_grad, (((0,), (0,)), ((), ())), preferred_element_type=jnp.float32)
    return (attended.reshape(SAMPLES, TOKENS, head_width), query_grad.reshape(SAMPLES, TOKENS, head_width), feature_grad, weight_grad)
```

```python
import functools
import math

import jax
import jax.numpy as jnp
from jax import lax
from jax.experimental import pallas as pl
from jax.experimental.pallas import tpu as pltpu
from jax.sharding import PartitionSpec as P

HEAD_DIM = 128
WINDOW = 2048
LANES = 4
SCORE_SCALE = 1.0 / math.sqrt(HEAD_DIM)
EXP2_SCALE = SCORE_SCALE * math.log2(math.e)
MASKED = -1e30
MINOR_DIMS = (((1,), (1,)), ((), ()))
MAJOR_DIMS = (((0,), (0,)), ((), ()))


def exchanged(value, bits):
    count = lax.axis_size("seq")
    return lax.ppermute(value, "seq", [(source, source ^ bits) for source in range(count)])


def shifted(value, rows):
    count = lax.axis_size("seq")
    steps = rows * LANES
    leading, last = (max(0, -steps), min(count, count - steps))
    return lax.ppermute(value, "seq", [(source, source + steps) for source in range(leading, last)])


def swapped(value):
    return lax.ppermute(value, "dp", [(0, 1), (1, 0)])


def by_sublane(block, reduce):
    return reduce(block.reshape(block.shape[0] // 8, 8, block.shape[1]), axis=0)


def attention_kernel(
    row_ref, qu_ref, far_ref, near_ref, own_ref,
    out_ref, far_grad_ref, near_grad_ref, own_grad_ref,
    window, turned, total, scores, dprobs,
    *, blocks, span, size,
):
    step = pl.program_id(1)
    row_tokens = blocks * size

    @pl.when(step == 0)
    def _():
        window[:row_tokens] = far_ref[...]
        window[row_tokens : 2 * row_tokens] = near_ref[...]
        window[2 * row_tokens :] = own_ref[...]
        total[...] = jnp.zeros_like(total)
        for block in range(3 * blocks):
            turned[block] = window[block * size : (block + 1) * size].T

    query = qu_ref[0]
    cotangent = qu_ref[1]
    first = row_ref[0] * blocks + step - span
    key_pos = lax.broadcasted_iota(jnp.int32, (size, size), 0)
    query_pos = lax.broadcasted_iota(jnp.int32, (size, size), 1)

    def rows_of(block):
        return pl.ds((step + block) * size, size)

    peak = jnp.full((8, size), MASKED, jnp.float32)
    for block in range(span + 1):
        key = window[rows_of(block), :HEAD_DIM]
        score = lax.dot_general(key, query, MINOR_DIMS, preferred_element_type=jnp.float32)
        if block == span:
            allowed = key_pos <= query_pos
        elif block == 0:
            allowed = (key_pos > query_pos) & (first >= 0)
        else:
            allowed = first + block >= 0
        score = jnp.where(allowed, score, MASKED)
        scores[block * size : (block + 1) * size] = score
        peak = jnp.maximum(peak, by_sublane(score, jnp.max))
    peak = jnp.max(peak, axis=0, keepdims=True)
    mass = jnp.zeros((8, size), jnp.float32)
    pull = jnp.zeros((8, size), jnp.float32)
    for block in range(span + 1):
        value = window[rows_of(block), HEAD_DIM:]
        held = slice(block * size, (block + 1) * size)
        grown = jnp.exp2((scores[held] - peak) * EXP2_SCALE)
        dprob = lax.dot_general(value, cotangent, MINOR_DIMS, preferred_element_type=jnp.float32)
        mass = mass + by_sublane(grown, jnp.sum)
        pull = pull + by_sublane(grown * dprob, jnp.sum)
        scores[held] = grown
        dprobs[held] = dprob
    share = 1.0 / jnp.sum(mass, axis=0, keepdims=True)
    centre = jnp.sum(pull, axis=0, keepdims=True) * share
    attended = jnp.zeros((HEAD_DIM, size), jnp.float32)
    query_grad = jnp.zeros((HEAD_DIM, size), jnp.float32)
    for block in range(span + 1):
        held = slice(block * size, (block + 1) * size)
        probability = scores[held] * share
        weights = probability.astype(jnp.bfloat16)
        dscore = (probability * (dprobs[held] - centre) * SCORE_SCALE).astype(jnp.bfloat16)
        key_turned = turned[step + block, :HEAD_DIM]
        value_turned = turned[step + block, HEAD_DIM:]
        attended += jnp.dot(value_turned, weights, preferred_element_type=jnp.float32)
        query_grad += jnp.dot(key_turned, dscore, preferred_element_type=jnp.float32)
        total[rows_of(block), :HEAD_DIM] += jnp.dot(
            dscore, query, preferred_element_type=jnp.float32
        )
        total[rows_of(block), HEAD_DIM:] += jnp.dot(
            weights, cotangent, preferred_element_type=jnp.float32
        )
    out_ref[0] = attended.T.astype(jnp.bfloat16)
    out_ref[1] = query_grad.T.astype(jnp.bfloat16)

    @pl.when(step == blocks - 1)
    def _():
        far_grad_ref[...] = total[:row_tokens].astype(jnp.bfloat16)
        near_grad_ref[...] = total[row_tokens : 2 * row_tokens]
        own_grad_ref[...] = total[2 * row_tokens :]


def attention(row, query_pair, far, near, own, size):
    _, row_tokens, width = query_pair.shape
    heads = width // HEAD_DIM
    blocks = row_tokens // size
    span = WINDOW // size
    pair_spec = pl.BlockSpec((2, size, HEAD_DIM), lambda head, step, *_: (0, step, head))
    kv_spec = pl.BlockSpec((row_tokens, 2 * HEAD_DIM), lambda head, step, *_: (0, head))
    kv_shape = (row_tokens, 2 * width)
    cells = heads * row_tokens * (span + 1) * size
    return pl.pallas_call(
        functools.partial(attention_kernel, blocks=blocks, span=span, size=size),
        grid_spec=pltpu.PrefetchScalarGridSpec(
            num_scalar_prefetch=1,
            grid=(heads, blocks),
            in_specs=[pair_spec, kv_spec, kv_spec, kv_spec],
            out_specs=[pair_spec, kv_spec, kv_spec, kv_spec],
            scratch_shapes=[
                pltpu.VMEM((3 * row_tokens, 2 * HEAD_DIM), jnp.bfloat16),
                pltpu.VMEM((3 * blocks, 2 * HEAD_DIM, size), jnp.bfloat16),
                pltpu.VMEM((3 * row_tokens, 2 * HEAD_DIM), jnp.float32),
                pltpu.VMEM(((span + 1) * size, size), jnp.float32),
                pltpu.VMEM(((span + 1) * size, size), jnp.float32),
            ],
        ),
        out_shape=[
            jax.ShapeDtypeStruct(query_pair.shape, jnp.bfloat16),
            jax.ShapeDtypeStruct(kv_shape, jnp.bfloat16),
            jax.ShapeDtypeStruct(kv_shape, jnp.float32),
            jax.ShapeDtypeStruct(kv_shape, jnp.float32),
        ],
        compiler_params=pltpu.CompilerParams(vmem_limit_bytes=48 * 2**20),
        cost_estimate=pl.CostEstimate(
            flops=12 * cells * HEAD_DIM, bytes_accessed=9 * 2**20, transcendentals=cells
        ),
        name="window_attention",
    )(row, query_pair, far, near, own)


def placed(pieces, lane, axis):
    size = pieces[0].shape[axis]
    shape = list(pieces[0].shape)
    shape[axis] = size * LANES
    whole = jnp.zeros(shape, pieces[0].dtype)
    for bits, piece in enumerate(pieces):
        whole = lax.dynamic_update_slice_in_dim(whole, piece, (lane ^ bits) * size, axis)
    return whole


def dealt(value, lane, axis):
    size = value.shape[axis] // LANES
    pieces = []
    for bits in range(LANES):
        piece = lax.dynamic_slice_in_dim(value, (lane ^ bits) * size, size, axis)
        pieces.append(exchanged(piece, bits) if bits else piece)
    return pieces


def local(features, queries, kv_weight, upstream):
    tokens = features[0]
    size = tokens.shape[0]
    weight_rows, kv_width = kv_weight.shape
    width = kv_width // 2
    lane_width = width // LANES
    heads = lane_width // HEAD_DIM
    rows = lax.axis_size("seq") // LANES
    place = lax.axis_index("seq")
    lane = place % LANES
    row = place // LANES
    half = lax.axis_index("dp")
    core = place % 2

    key_cols = lax.dynamic_slice_in_dim(kv_weight, lane * lane_width, lane_width, 1)
    value_cols = lax.dynamic_slice_in_dim(kv_weight, width + lane * lane_width, lane_width, 1)
    lane_weight = jnp.concatenate(
        [
            part[:, head * HEAD_DIM : (head + 1) * HEAD_DIM]
            for head in range(heads)
            for part in (key_cols, value_cols)
        ],
        axis=1,
    )
    other_lane_weight = swapped(lane_weight)
    across = exchanged(tokens, 2)
    beside = exchanged(tokens, 1)
    diagonal = exchanged(across, 1)
    row_tokens = placed([tokens, beside, across, diagonal], lane, 0)
    whole_weight = jnp.zeros((2 * weight_rows, lane_weight.shape[1]), jnp.bfloat16)
    whole_weight = lax.dynamic_update_slice_in_dim(whole_weight, lane_weight, half * weight_rows, 0)
    whole_weight = lax.dynamic_update_slice_in_dim(
        whole_weight, other_lane_weight, (1 - half) * weight_rows, 0
    )
    own = jnp.dot(row_tokens, whole_weight, preferred_element_type=jnp.float32).astype(jnp.bfloat16)
    near = shifted(own, 1)
    far = shifted(near, 1)

    query_pair = placed(dealt(jnp.concatenate([queries, upstream], 0), lane, 2), lane, 1)

    part_rows = weight_rows // 2
    fetched = swapped(lax.dynamic_slice_in_dim(kv_weight, core * part_rows, part_rows, 0))
    passed = exchanged(fetched, 1)

    out_pair, far_grad, near_grad, own_grad = attention(
        row[None], query_pair, far, near, own, size
    )
    carried = shifted(far_grad, -1).astype(jnp.float32)
    carried = shifted((near_grad + carried).astype(jnp.bfloat16), -1).astype(jnp.float32)
    kv_grad = (own_grad + carried).astype(jnp.bfloat16)

    out_pair = placed(dealt(out_pair, lane, 1), lane, 2)

    lane_grads = dealt(kv_grad, lane, 0)
    token_grad = placed([piece[:, None] for piece in lane_grads], lane, 1)
    token_grad = (
        token_grad.reshape(size, LANES, heads, 2, HEAD_DIM)
        .transpose(0, 3, 1, 2, 4)
        .reshape(size, kv_width)
    )

    def against(weight):
        return lax.dot_general(
            token_grad, weight, MINOR_DIMS, preferred_element_type=jnp.float32
        ).astype(jnp.bfloat16)

    feature_grad = jnp.zeros((size, 2 * weight_rows), jnp.bfloat16)
    for piece, start in (
        (kv_weight, half * weight_rows),
        (fetched, (1 - half) * weight_rows + core * part_rows),
        (passed, (1 - half) * weight_rows + (1 - core) * part_rows),
    ):
        feature_grad = lax.dynamic_update_slice_in_dim(feature_grad, against(piece), start, 1)

    partial = lax.dot_general(row_tokens, kv_grad, MAJOR_DIMS, preferred_element_type=jnp.float32)

    def halved(pairs, bit, send):
        kept = lax.dynamic_index_in_dim(pairs, bit, 1, keepdims=False)
        given = lax.dynamic_index_in_dim(pairs, 1 - bit, 1, keepdims=False)
        return kept + send(given.astype(jnp.bfloat16)).astype(jnp.float32)

    lane_cols = partial.shape[1]
    partial = halved(partial.reshape(1, 2, weight_rows, lane_cols), half, swapped)
    partial = partial.reshape(rows, weight_rows // rows, lane_cols)
    distance = 1
    while distance < rows:
        partial = halved(
            partial.reshape(partial.shape[0] // 2, 2, weight_rows // rows, lane_cols),
            (row // distance) % 2,
            functools.partial(exchanged, bits=distance * LANES),
        )
        distance *= 2
    pieces = dealt(partial[0], lane, 0)
    weight_grad = placed([piece[:, None] for piece in pieces], lane, 1)
    weight_grad = (
        weight_grad.reshape(-1, LANES, heads, 2, HEAD_DIM)
        .transpose(0, 3, 1, 2, 4)
        .reshape(-1, kv_width)
    )
    return (out_pair[:1], out_pair[1:], feature_grad[None], weight_grad)


def solution(mesh):
    return jax.shard_map(
        local,
        mesh=mesh,
        in_specs=(P("dp", "seq", None), P("dp", "seq", None), P("dp", None), P("dp", "seq", None)),
        out_specs=(
            P("dp", "seq", None),
            P("dp", "seq", None),
            P("dp", "seq", None),
            P(("dp", "seq"), None),
        ),
        check_vma=False,
    )
```

```python
import functools
import math

import jax
import jax.numpy as jnp
from jax import lax
from jax.experimental import pallas as pl
from jax.experimental.pallas import tpu as pltpu
from jax.sharding import PartitionSpec as P

HEAD_DIM = 128
WINDOW = 2048
LANES = 4
SCORE_SCALE = 1.0 / math.sqrt(HEAD_DIM)
EXP2_SCALE = SCORE_SCALE * math.log2(math.e)
MASKED = -1e30
MINOR_DIMS = (((1,), (1,)), ((), ()))
MAJOR_DIMS = (((0,), (0,)), ((), ()))


def exchanged(value, bits):
    count = lax.axis_size("seq")
    return lax.ppermute(value, "seq", [(source, source ^ bits) for source in range(count)])


def shifted(value, rows):
    count = lax.axis_size("seq")
    steps = rows * LANES
    leading, last = (max(0, -steps), min(count, count - steps))
    return lax.ppermute(value, "seq", [(source, source + steps) for source in range(leading, last)])


def swapped(value):
    return lax.ppermute(value, "dp", [(0, 1), (1, 0)])


def after(value, *others):
    return lax.optimization_barrier((value, *others))[0]


def by_sublane(block, reduce):
    return reduce(block.reshape(block.shape[0] // 8, 8, block.shape[1]), axis=0)


def attention_kernel(
    row_ref, qu_ref, far_ref, near_ref, own_ref,
    out_ref, far_grad_ref, near_grad_ref, own_grad_ref,
    window, turned, total, scores, dprobs,
    *, blocks, span, size,
):
    step = pl.program_id(0)
    row_tokens = blocks * size

    @pl.when(step == 0)
    def _():
        window[:row_tokens] = far_ref[...]
        window[row_tokens : 2 * row_tokens] = near_ref[...]
        window[2 * row_tokens :] = own_ref[...]
        total[...] = jnp.zeros_like(total)
        for block in range(3 * blocks):
            turned[block] = window[block * size : (block + 1) * size].T

    query = qu_ref[0]
    cotangent = qu_ref[1]
    first = row_ref[0] * blocks + step - span
    key_pos = lax.broadcasted_iota(jnp.int32, (size, size), 0)
    query_pos = lax.broadcasted_iota(jnp.int32, (size, size), 1)

    def rows_of(block):
        return pl.ds((step + block) * size, size)

    peak = jnp.full((8, size), MASKED, jnp.float32)
    for block in range(span + 1):
        key = window[rows_of(block), :HEAD_DIM]
        score = lax.dot_general(key, query, MINOR_DIMS, preferred_element_type=jnp.float32)
        if block == span:
            allowed = key_pos <= query_pos
        elif block == 0:
            allowed = (key_pos > query_pos) & (first >= 0)
        else:
            allowed = first + block >= 0
        score = jnp.where(allowed, score, MASKED)
        scores[block * size : (block + 1) * size] = score
        peak = jnp.maximum(peak, by_sublane(score, jnp.max))
    peak = jnp.max(peak, axis=0, keepdims=True)
    mass = jnp.zeros((8, size), jnp.float32)
    pull = jnp.zeros((8, size), jnp.float32)
    for block in range(span + 1):
        value = window[rows_of(block), HEAD_DIM:]
        held = slice(block * size, (block + 1) * size)
        grown = jnp.exp2((scores[held] - peak) * EXP2_SCALE)
        dprob = lax.dot_general(value, cotangent, MINOR_DIMS, preferred_element_type=jnp.float32)
        mass = mass + by_sublane(grown, jnp.sum)
        pull = pull + by_sublane(grown * dprob, jnp.sum)
        scores[held] = grown
        dprobs[held] = dprob
    share = 1.0 / jnp.sum(mass, axis=0, keepdims=True)
    centre = jnp.sum(pull, axis=0, keepdims=True) * share
    attended = jnp.zeros((HEAD_DIM, size), jnp.float32)
    query_grad = jnp.zeros((HEAD_DIM, size), jnp.float32)
    for block in range(span + 1):
        held = slice(block * size, (block + 1) * size)
        probability = scores[held] * share
        weights = probability.astype(jnp.bfloat16)
        dscore = (probability * (dprobs[held] - centre) * SCORE_SCALE).astype(jnp.bfloat16)
        key_turned = turned[step + block, :HEAD_DIM]
        value_turned = turned[step + block, HEAD_DIM:]
        attended += jnp.dot(value_turned, weights, preferred_element_type=jnp.float32)
        query_grad += jnp.dot(key_turned, dscore, preferred_element_type=jnp.float32)
        total[rows_of(block), :HEAD_DIM] += jnp.dot(
            dscore, query, preferred_element_type=jnp.float32
        )
        total[rows_of(block), HEAD_DIM:] += jnp.dot(
            weights, cotangent, preferred_element_type=jnp.float32
        )
    out_ref[0] = attended.T.astype(jnp.bfloat16)
    out_ref[1] = query_grad.T.astype(jnp.bfloat16)

    @pl.when(step == blocks - 1)
    def _():
        far_grad_ref[...] = total[:row_tokens].astype(jnp.bfloat16)
        near_grad_ref[...] = total[row_tokens : 2 * row_tokens]
        own_grad_ref[...] = total[2 * row_tokens :]


def attention(row, query_pair, head, far, near, own, size):
    row_tokens = query_pair.shape[1]
    blocks = row_tokens // size
    span = WINDOW // size
    pair_in = pl.BlockSpec((2, size, HEAD_DIM), lambda step, *_: (0, step, head))
    pair_out = pl.BlockSpec((2, size, HEAD_DIM), lambda step, *_: (0, step, 0))
    kv_shape = (row_tokens, 2 * HEAD_DIM)
    kv_spec = pl.BlockSpec(kv_shape, lambda step, *_: (0, 0))
    cells = row_tokens * (span + 1) * size
    return pl.pallas_call(
        functools.partial(attention_kernel, blocks=blocks, span=span, size=size),
        grid_spec=pltpu.PrefetchScalarGridSpec(
            num_scalar_prefetch=1,
            grid=(blocks,),
            in_specs=[pair_in, kv_spec, kv_spec, kv_spec],
            out_specs=[pair_out, kv_spec, kv_spec, kv_spec],
            scratch_shapes=[
                pltpu.VMEM((3 * row_tokens, 2 * HEAD_DIM), jnp.bfloat16),
                pltpu.VMEM((3 * blocks, 2 * HEAD_DIM, size), jnp.bfloat16),
                pltpu.VMEM((3 * row_tokens, 2 * HEAD_DIM), jnp.float32),
                pltpu.VMEM(((span + 1) * size, size), jnp.float32),
                pltpu.VMEM(((span + 1) * size, size), jnp.float32),
            ],
        ),
        out_shape=[
            jax.ShapeDtypeStruct((2, row_tokens, HEAD_DIM), jnp.bfloat16),
            jax.ShapeDtypeStruct(kv_shape, jnp.bfloat16),
            jax.ShapeDtypeStruct(kv_shape, jnp.float32),
            jax.ShapeDtypeStruct(kv_shape, jnp.float32),
        ],
        compiler_params=pltpu.CompilerParams(vmem_limit_bytes=48 * 2**20),
        cost_estimate=pl.CostEstimate(
            flops=12 * cells * HEAD_DIM, bytes_accessed=5 * 2**20, transcendentals=cells
        ),
        name="window_attention",
    )(row, query_pair, far, near, own)


def placed(pieces, lane, axis):
    size = pieces[0].shape[axis]
    shape = list(pieces[0].shape)
    shape[axis] = size * LANES
    whole = jnp.zeros(shape, pieces[0].dtype)
    for bits, piece in enumerate(pieces):
        whole = lax.dynamic_update_slice_in_dim(whole, piece, (lane ^ bits) * size, axis)
    return whole


def dealt(value, lane, axis):
    size = value.shape[axis] // LANES
    pieces = []
    for bits in range(LANES):
        piece = lax.dynamic_slice_in_dim(value, (lane ^ bits) * size, size, axis)
        pieces.append(exchanged(piece, bits) if bits else piece)
    return pieces


def local(features, queries, kv_weight, upstream):
    tokens = features[0]
    size = tokens.shape[0]
    weight_rows, kv_width = kv_weight.shape
    width = kv_width // 2
    lane_width = width // LANES
    heads = lane_width // HEAD_DIM
    rows = lax.axis_size("seq") // LANES
    place = lax.axis_index("seq")
    lane = place % LANES
    row = place // LANES
    half = lax.axis_index("dp")
    core = place % 2

    key_cols = lax.dynamic_slice_in_dim(kv_weight, lane * lane_width, lane_width, 1)
    value_cols = lax.dynamic_slice_in_dim(kv_weight, width + lane * lane_width, lane_width, 1)
    lane_weight = jnp.concatenate(
        [
            part[:, head * HEAD_DIM : (head + 1) * HEAD_DIM]
            for head in range(heads)
            for part in (key_cols, value_cols)
        ],
        axis=1,
    )
    other_lane_weight = swapped(lane_weight)
    across = exchanged(tokens, 2)
    beside = exchanged(tokens, 1)
    diagonal = exchanged(across, 1)
    row_tokens = placed([tokens, beside, across, diagonal], lane, 0)
    whole_weight = jnp.zeros((2 * weight_rows, lane_weight.shape[1]), jnp.bfloat16)
    whole_weight = lax.dynamic_update_slice_in_dim(whole_weight, lane_weight, half * weight_rows, 0)
    whole_weight = lax.dynamic_update_slice_in_dim(
        whole_weight, other_lane_weight, (1 - half) * weight_rows, 0
    )
    owns, nears, fars = [], [], []
    for head in range(heads):
        head_weight = whole_weight[:, head * 2 * HEAD_DIM : (head + 1) * 2 * HEAD_DIM]
        if head:
            head_weight = after(head_weight, nears[-1])
        own = jnp.dot(row_tokens, head_weight, preferred_element_type=jnp.float32)
        own = own.astype(jnp.bfloat16)
        owns.append(own)
        nears.append(shifted(own, 1))
        fars.append(shifted(nears[-1], 1))

    query_pair = placed(dealt(jnp.concatenate([queries, upstream], 0), lane, 2), lane, 1)

    part_rows = weight_rows // 2
    fetched = swapped(lax.dynamic_slice_in_dim(kv_weight, core * part_rows, part_rows, 0))
    passed = exchanged(fetched, 1)

    out_pairs, kv_grads = [], []
    for head in range(heads):
        out_pair, far_grad, near_grad, own_grad = attention(
            row[None], query_pair, head, fars[head], nears[head], owns[head], size
        )
        out_pairs.append(out_pair)
        carried = shifted(far_grad, -1).astype(jnp.float32)
        carried = shifted((near_grad + carried).astype(jnp.bfloat16), -1).astype(jnp.float32)
        kv_grads.append((own_grad + carried).astype(jnp.bfloat16))

    out_pair = placed(dealt(jnp.concatenate(out_pairs, 2), lane, 1), lane, 2)

    token_grad = jnp.stack(
        [
            placed([piece[:, None] for piece in dealt(kv_grad, lane, 0)], lane, 1)
            for kv_grad in kv_grads
        ],
        2,
    )
    token_grad = (
        token_grad.reshape(size, LANES, heads, 2, HEAD_DIM)
        .transpose(0, 3, 1, 2, 4)
        .reshape(size, kv_width)
    )

    def against(weight):
        return lax.dot_general(
            token_grad, weight, MINOR_DIMS, preferred_element_type=jnp.float32
        ).astype(jnp.bfloat16)

    feature_grad = jnp.zeros((size, 2 * weight_rows), jnp.bfloat16)
    for piece, start in (
        (kv_weight, half * weight_rows),
        (fetched, (1 - half) * weight_rows + core * part_rows),
        (passed, (1 - half) * weight_rows + (1 - core) * part_rows),
    ):
        feature_grad = lax.dynamic_update_slice_in_dim(feature_grad, against(piece), start, 1)

    def halved(pairs, bit, send):
        kept = lax.dynamic_index_in_dim(pairs, bit, 1, keepdims=False)
        given = lax.dynamic_index_in_dim(pairs, 1 - bit, 1, keepdims=False)
        return kept + send(given.astype(jnp.bfloat16)).astype(jnp.float32)

    weight_grads = []
    for kv_grad in kv_grads:
        partial = lax.dot_general(
            row_tokens, kv_grad, MAJOR_DIMS, preferred_element_type=jnp.float32
        )
        cols = partial.shape[1]
        partial = halved(partial.reshape(1, 2, weight_rows, cols), half, swapped)
        partial = partial.reshape(rows, weight_rows // rows, cols)
        distance = 1
        while distance < rows:
            partial = halved(
                partial.reshape(partial.shape[0] // 2, 2, weight_rows // rows, cols),
                (row // distance) % 2,
                functools.partial(exchanged, bits=distance * LANES),
            )
            distance *= 2
        pieces = dealt(partial[0], lane, 0)
        weight_grads.append(placed([piece[:, None] for piece in pieces], lane, 1))
    weight_grad = (
        jnp.stack(weight_grads, 2)
        .reshape(-1, LANES, heads, 2, HEAD_DIM)
        .transpose(0, 3, 1, 2, 4)
        .reshape(-1, kv_width)
    )
    return (out_pair[:1], out_pair[1:], feature_grad[None], weight_grad)


def solution(mesh):
    return jax.shard_map(
        local,
        mesh=mesh,
        in_specs=(P("dp", "seq", None), P("dp", "seq", None), P("dp", None), P("dp", "seq", None)),
        out_specs=(
            P("dp", "seq", None),
            P("dp", "seq", None),
            P("dp", "seq", None),
            P(("dp", "seq"), None),
        ),
        check_vma=False,
    )
```

```python
import functools
import math

import jax
import jax.numpy as jnp
from jax import lax
from jax.experimental import pallas as pl
from jax.experimental.pallas import tpu as pltpu
from jax.sharding import PartitionSpec as P

HEAD_DIM = 128
WINDOW = 2048
LANES = 4
VMEM_GRANT = 24 * 2**20
SCORE_SCALE = 1.0 / math.sqrt(HEAD_DIM)
EXP2_SCALE = SCORE_SCALE * math.log2(math.e)
MASKED = -1e30
MINOR_DIMS = (((1,), (1,)), ((), ()))
MAJOR_DIMS = (((0,), (0,)), ((), ()))


def exchanged(value, bits):
    count = lax.axis_size("seq")
    return lax.ppermute(value, "seq", [(source, source ^ bits) for source in range(count)])


def shifted(value, rows):
    count = lax.axis_size("seq")
    steps = rows * LANES
    leading, last = (max(0, -steps), min(count, count - steps))
    return lax.ppermute(value, "seq", [(source, source + steps) for source in range(leading, last)])


def turned_round(value, rows):
    count = lax.axis_size("seq")
    pairs = [(source, (source + rows * LANES) % count) for source in range(count)]
    return lax.ppermute(value, "seq", pairs)


def moved(value, bits, across):
    count = lax.axis_size("seq")
    pairs = [
        (2 * place + side, 2 * (place ^ bits) + (side ^ across))
        for place in range(count)
        for side in range(2)
    ]
    return lax.ppermute(value, ("seq", "dp"), pairs)


def swapped(value):
    return lax.ppermute(value, "dp", [(0, 1), (1, 0)])


def by_sublane(block, reduce):
    return reduce(block.reshape(block.shape[0] // 8, 8, block.shape[1]), axis=0)


def product(left, right):
    return jnp.dot(left, right, preferred_element_type=jnp.float32)


def product_minor(left, right):
    return lax.dot_general(left, right, MINOR_DIMS, preferred_element_type=jnp.float32)


def take_kernel(_, weight_ref, out_ref):
    out_ref[...] = weight_ref[...]


def take_columns(at, weight, waits):
    depth, width = weight.shape
    columns = width // HEAD_DIM
    heads = columns // 2 // LANES

    def source(index, at_ref):
        return (0, index % 2 * (columns // 2) + at_ref[0] * heads + index // 2)

    return pl.pallas_call(
        ordered(take_kernel, 1, len(waits), 1, 0),
        grid_spec=pltpu.PrefetchScalarGridSpec(
            num_scalar_prefetch=1,
            grid=(2 * heads,),
            in_specs=[pl.BlockSpec((depth, HEAD_DIM), source)]
            + [pl.BlockSpec(memory_space=pl.ANY)] * len(waits),
            out_specs=pl.BlockSpec((depth, HEAD_DIM), lambda index, _: (0, index)),
        ),
        out_shape=jax.ShapeDtypeStruct((depth, 2 * heads * HEAD_DIM), weight.dtype),
        compiler_params=pltpu.CompilerParams(vmem_limit_bytes=VMEM_GRANT),
        cost_estimate=time_estimate(1),
        name="take_columns",
    )(at, weight, *waits)


def project_kernel(at_ref, *refs, heads):
    tokens, here_ref, there_ref, outs = refs[:LANES], refs[LANES], refs[LANES + 1], refs[-heads:]
    lane, half = at_ref[0], at_ref[1]
    depth = here_ref.shape[0]
    for bits, piece in enumerate(tokens):
        here = piece[:, at_offset(half, depth)]
        there = piece[:, at_offset(1 - half, depth)]
        whole = product(here, here_ref[...]) + product(there, there_ref[...])
        held = at_offset(lane ^ bits, piece.shape[0])
        width = whole.shape[1] // heads
        for head, out in enumerate(outs):
            out[held] = whole[:, head * width : (head + 1) * width].astype(jnp.bfloat16)


def project(at, tokens, weights):
    heads = weights[0].shape[1] // (2 * HEAD_DIM)
    whole = jax.ShapeDtypeStruct((LANES * tokens[0].shape[0], 2 * HEAD_DIM), jnp.bfloat16)
    return small_call(
        functools.partial(project_kernel, heads=heads),
        "project", at, (*tokens, *weights), [whole] * heads, cost=4,
    )


def visits(blocks):
    for turn in range(blocks):
        whole = [(1, lane, None) for lane in range(blocks)]
        yield 0, turn, whole + [(0, lane, "low" if lane == turn else None) for lane in range(turn + 1)]
        yield 1, turn, [(1, lane, "high" if lane == turn else None) for lane in range(turn, blocks)]


def masked(score, near, edge, near_bias):
    if edge:
        key_pos = lax.broadcasted_iota(jnp.int32, score.shape, 0)
        query_pos = lax.broadcasted_iota(jnp.int32, score.shape, 1)
        allowed = key_pos <= query_pos if edge == "low" else key_pos > query_pos
        score = jnp.where(allowed, score, MASKED)
    return score + near_bias if near else score


def stats_kernel(
    at_ref, own_pair, next_pair, own_ref, near_ref, own_out, next_out, scores, *, blocks, size
):
    near_bias = jnp.where(at_ref[0] > 0, 0.0, MASKED)
    window = (own_ref, near_ref)
    pairs = (own_pair, next_pair)
    outs = (own_out, next_out)
    for turn, (side, block, keys) in enumerate(visits(blocks)):
        held = slice(block * size, (block + 1) * size)
        peak = jnp.full((8, size), MASKED, jnp.float32)
        for index, (near, lane, edge) in enumerate(keys):
            key = window[near][lane * size : (lane + 1) * size, :HEAD_DIM]
            score = masked(product_minor(key, pairs[side][0, held]), near, edge, near_bias)
            scores[turn % 2, index] = score
            peak = jnp.maximum(peak, by_sublane(score, jnp.max))
        peak = jnp.max(peak, axis=0, keepdims=True)
        mass = jnp.zeros((8, size), jnp.float32)
        pull = jnp.zeros((8, size), jnp.float32)
        for index, (near, lane, edge) in enumerate(keys):
            value = window[near][lane * size : (lane + 1) * size, HEAD_DIM:]
            grown = jnp.exp2((scores[turn % 2, index] - peak) * EXP2_SCALE)
            mass = mass + by_sublane(grown, jnp.sum)
            pull = pull + by_sublane(grown * product_minor(value, pairs[side][1, held]), jnp.sum)
        out = outs[side]
        out[0:1, held] = peak
        out[1:2, held] = jnp.sum(mass, axis=0, keepdims=True)
        out[2:3, held] = jnp.sum(pull, axis=0, keepdims=True)
        out[3:, held] = jnp.zeros((5, size), jnp.float32)


def settled(here, there, there_valid):
    here_peak = here[0:1]
    there_peak = jnp.where(there_valid, there[0:1], MASKED)
    peak = jnp.maximum(here_peak, there_peak)
    here_factor = jnp.exp2((here_peak - peak) * EXP2_SCALE)
    there_factor = jnp.exp2((there_peak - peak) * EXP2_SCALE)
    mass = here[1:2] * here_factor + there[1:2] * there_factor
    pull = here[2:3] * here_factor + there[2:3] * there_factor
    share = jnp.where(mass > 0, 1.0 / mass, 0.0)
    return peak, share, pull * share


def gradient_kernel(
    at_ref, own_pair, next_pair, own_ref, near_ref,
    own_stats, far_stats, next_stats, main_stats,
    own_out, next_out, near_grad, own_grad,
    turned, queries, cotangents, own_weights, own_dscores, near_weights, near_dscores,
    *, blocks, size,
):
    near_valid = at_ref[0] > 0
    near_bias = jnp.where(near_valid, 0.0, MASKED)
    window = (own_ref, near_ref)
    row_tokens = blocks * size
    pairs = (own_pair, next_pair)
    outs = (own_out, next_out)
    weights = (own_weights, near_weights)
    dscores = (own_dscores, near_dscores)
    figures = (
        settled(own_stats[...], far_stats[...], near_valid),
        settled(next_stats[...], main_stats[...], True),
    )
    for side in range(2):
        queries[side * row_tokens : (side + 1) * row_tokens] = pairs[side][0]
        cotangents[side * row_tokens : (side + 1) * row_tokens] = pairs[side][1]
        for block in range(blocks):
            held = slice(block * size, (block + 1) * size)
            turned[side, :, held] = window[side][held].T
    for side, block, keys in visits(blocks):
        held = slice(block * size, (block + 1) * size)
        column = slice(side * row_tokens + block * size, side * row_tokens + (block + 1) * size)
        peak, share, centre = (figure[:, held] for figure in figures[side])
        scaled = share * SCORE_SCALE
        for near, lane, edge in keys:
            rows = slice(lane * size, (lane + 1) * size)
            score = product_minor(window[near][rows, :HEAD_DIM], pairs[side][0, held])
            dprob = product_minor(window[near][rows, HEAD_DIM:], pairs[side][1, held])
            grown = jnp.exp2((masked(score, near, edge, near_bias) - peak) * EXP2_SCALE)
            weights[near][rows, column] = (grown * share).astype(jnp.bfloat16)
            dscores[near][rows, column] = (grown * ((dprob - centre) * scaled)).astype(jnp.bfloat16)
        rows = slice(block * size if side else 0, row_tokens)
        attended = product(turned[1, HEAD_DIM:, rows], near_weights[rows, column])
        query_grad = product(turned[1, :HEAD_DIM, rows], near_dscores[rows, column])
        if not side:
            rows = slice(0, (block + 1) * size)
            attended += product(turned[0, HEAD_DIM:, rows], own_weights[rows, column])
            query_grad += product(turned[0, :HEAD_DIM, rows], own_dscores[rows, column])
        outs[side][0, held] = attended.T.astype(outs[side].dtype)
        outs[side][1, held] = query_grad.T.astype(outs[side].dtype)
    for lane in range(blocks):
        rows = slice(lane * size, (lane + 1) * size)
        met = slice(0, row_tokens + (lane + 1) * size)
        near_grad[rows, :HEAD_DIM] = product(near_dscores[rows, met], queries[met]).astype(
            jnp.bfloat16
        )
        near_grad[rows, HEAD_DIM:] = product(near_weights[rows, met], cotangents[met]).astype(
            jnp.bfloat16
        )
        met = slice(lane * size, row_tokens)
        own_grad[rows, :HEAD_DIM] = product(own_dscores[rows, met], queries[met])
        own_grad[rows, HEAD_DIM:] = product(own_weights[rows, met], cotangents[met])


def kernel_call(kernel, name, at, own_pair, next_pair, kvs, stats, out_shape, scratch, size, waits, cost, grant):
    row_tokens = own_pair.shape[1]
    blocks = row_tokens // size

    return pl.pallas_call(
        ordered(
            functools.partial(kernel, blocks=blocks, size=size),
            2 + len(kvs) + len(stats),
            len(waits),
            len(out_shape),
            0,
        ),
        grid_spec=pltpu.PrefetchScalarGridSpec(
            num_scalar_prefetch=1,
            grid=(1,),
            in_specs=[whole_block(value) for value in (own_pair, next_pair, *kvs, *stats)]
            + [pl.BlockSpec(memory_space=pl.ANY)] * len(waits),
            out_specs=[whole_block(value) for value in out_shape],
            scratch_shapes=scratch,
        ),
        out_shape=out_shape,
        compiler_params=pltpu.CompilerParams(vmem_limit_bytes=grant),
        cost_estimate=time_estimate(cost),
        name=name,
    )(at, own_pair, next_pair, *kvs, *stats, *waits)


def softmax_stats(at, own_pair, next_pair, kvs, size):
    row_tokens = own_pair.shape[1]
    return kernel_call(
        stats_kernel, "softmax_stats", at, own_pair, next_pair, kvs, (),
        [jax.ShapeDtypeStruct((8, row_tokens), jnp.float32)] * 2,
        [pltpu.VMEM((2, 2 * row_tokens // size, size, size), jnp.float32)],
        size, (), 4, 16 * 2**20,
    )


def attention_grads(at, own_pair, next_pair, kvs, stats, size, waits):
    row_tokens = own_pair.shape[1]
    low = jnp.bfloat16
    return kernel_call(
        gradient_kernel, "attention_grads", at, own_pair, next_pair, kvs, stats,
        [
            jax.ShapeDtypeStruct((2, row_tokens, HEAD_DIM), jnp.float32),
            jax.ShapeDtypeStruct((2, row_tokens, HEAD_DIM), low),
            jax.ShapeDtypeStruct((row_tokens, 2 * HEAD_DIM), low),
            jax.ShapeDtypeStruct((row_tokens, 2 * HEAD_DIM), jnp.float32),
        ],
        [
            pltpu.VMEM((2, 2 * HEAD_DIM, row_tokens), low),
            pltpu.VMEM((2 * row_tokens, HEAD_DIM), low),
            pltpu.VMEM((2 * row_tokens, HEAD_DIM), low),
            pltpu.VMEM((row_tokens, row_tokens), low),
            pltpu.VMEM((row_tokens, row_tokens), low),
            pltpu.VMEM((row_tokens, 2 * row_tokens), low),
            pltpu.VMEM((row_tokens, 2 * row_tokens), low),
        ],
        size, waits, 8, 36 * 2**20,
    )


def at_offset(index, size):
    return pl.ds(pl.multiple_of(index * size, size), size)


def ordered(kernel, inputs, waits, outputs, through):
    def body(*refs):
        first = 1 + inputs + waits + through
        kept = first + outputs
        return kernel(*refs[: 1 + inputs], *refs[first:kept], *refs[kept + through :])

    return body


def time_estimate(microseconds):
    return pl.CostEstimate(
        flops=microseconds * 10**9, bytes_accessed=microseconds * 3 * 10**6, transcendentals=0
    )


def whole_block(value):
    return pl.BlockSpec(value.shape, lambda *_: (0,) * len(value.shape))


def small_call(
    kernel, name, at, operands, out_shape, scratch=(), waits=(), through=(), cost=1
):
    anywhere = pl.BlockSpec(memory_space=pl.ANY)
    first = 1 + len(operands) + len(waits)
    return pl.pallas_call(
        ordered(kernel, len(operands), len(waits), len(out_shape), len(through)),
        grid=(1,),
        in_specs=[pl.BlockSpec(memory_space=pltpu.SMEM)]
        + [whole_block(value) for value in operands]
        + [anywhere] * (len(waits) + len(through)),
        out_specs=[whole_block(value) for value in out_shape] + [anywhere] * len(through),
        out_shape=[
            *out_shape,
            *(jax.ShapeDtypeStruct(value.shape, value.dtype) for value in through),
        ],
        input_output_aliases={
            first + index: len(out_shape) + index for index in range(len(through))
        },
        scratch_shapes=list(scratch),
        compiler_params=pltpu.CompilerParams(vmem_limit_bytes=VMEM_GRANT),
        cost_estimate=time_estimate(cost),
        name=name,
    )(at, *operands, *waits, *through)


def mixed_kernel(_, held_ref, passed_ref, out):
    out[0] = held_ref[...]
    out[1] = passed_ref[1]


def go_round(at, pieces):
    own, held, given = pieces
    beside = exchanged(given, 1)
    shape = jax.ShapeDtypeStruct(given.shape, given.dtype)
    (both,) = small_call(mixed_kernel, "mix", at, (held, beside), [shape])
    across = exchanged(both, 2)
    return own, beside, across


def deal_kernel(at_ref, query_ref, cotangent_ref, *outs, heads):
    lane = at_ref[0]
    for head in range(heads):
        own, held, given = outs[3 * head : 3 * head + 3]
        for bits, out in enumerate((own, given.at[0], held, given.at[1])):
            column = at_offset((lane ^ bits) * heads + head, HEAD_DIM)
            out[0] = query_ref[0, :, column]
            out[1] = cotangent_ref[0, :, column]


def deal_heads(at, queries, upstream):
    _, size, width = queries.shape
    heads = width // LANES // HEAD_DIM
    piece = jax.ShapeDtypeStruct((2, size, HEAD_DIM), jnp.bfloat16)
    pair = jax.ShapeDtypeStruct((2, *piece.shape), jnp.bfloat16)
    outs = small_call(
        functools.partial(deal_kernel, heads=heads),
        "deal_heads", at, (queries, upstream), [piece, piece, pair] * heads,
    )
    return [outs[3 * head : 3 * head + 3] for head in range(heads)]


def place_rows_kernel(at_ref, own, beside, across, out):
    size = own.shape[1]
    for bits, piece in enumerate((own, beside.at[0], across.at[0], across.at[1])):
        out[:, at_offset(at_ref[0] ^ bits, size)] = piece[...]


def place_rows(at, found, waits, through):
    own, beside, across = found
    kinds, size, width = own.shape
    whole = jax.ShapeDtypeStruct((kinds, LANES * size, width), own.dtype)
    return small_call(
        place_rows_kernel, "place_rows", at, (own, beside, across), [whole],
        waits=waits, through=through,
    )


def settle_kernel(at_ref, own_out, arrived, own, held, given):
    size = own.shape[1]
    for bits, out in enumerate((own, given.at[0], held, given.at[1])):
        rows = at_offset(at_ref[0] ^ bits, size)
        out[...] = (own_out[:, rows] + arrived[:, rows].astype(jnp.float32)).astype(jnp.bfloat16)


def settle_out(at, own_out, arrived, waits):
    kinds, count, width = own_out.shape
    piece = jax.ShapeDtypeStruct((kinds, count // LANES, width), jnp.bfloat16)
    pair = jax.ShapeDtypeStruct((2, *piece.shape), jnp.bfloat16)
    return small_call(
        settle_kernel, "settle_out", at, (own_out, arrived), [piece, piece, pair], waits=waits
    )


def place_heads_kernel(at_ref, *refs, heads):
    outs = refs[3 * heads :]
    for head in range(heads):
        own, beside, across = refs[3 * head : 3 * head + 3]
        for bits, piece in enumerate((own, beside.at[0], across.at[0], across.at[1])):
            column = at_offset((at_ref[0] ^ bits) * heads + head, HEAD_DIM)
            for kind, out in enumerate(outs):
                out[0, :, column] = piece[kind]


def place_heads(at, found):
    heads = len(found)
    kinds, size, width = found[0][0].shape
    whole = jax.ShapeDtypeStruct((1, size, LANES * heads * width), jnp.bfloat16)
    return small_call(
        functools.partial(place_heads_kernel, heads=heads),
        "place_heads", at, [value for part in found for value in part],
        [whole] * kinds,
    )


def spread_kernel(at_ref, *refs, rows, before):
    tokens, own_ref, arrived_ref = refs[:LANES], refs[LANES], refs[LANES + 1]
    earlier = refs[LANES + 2 : LANES + 2 + before]
    own, held, given, kept_ref, sent_ref = refs[LANES + 2 + before : -2]
    kv_pieces = (own, given.at[0], held, given.at[1])
    if before:
        earlier = (earlier[0], earlier[2].at[0], earlier[1], earlier[2].at[1])
    turned, partial = refs[-2:]
    lane, half = at_ref[0], at_ref[1]
    size, depth = tokens[0].shape
    cols = own_ref.shape[1]
    for bits, piece in enumerate(kv_pieces):
        held = at_offset(lane ^ bits, size)
        kv_grad = (own_ref[held] + arrived_ref[held].astype(jnp.float32)).astype(jnp.bfloat16)
        if before:
            piece[:, : own.shape[1] - cols] = earlier[bits][...]
        piece[:, own.shape[1] - cols :] = kv_grad
        turned[:, bits * size : (bits + 1) * size] = kv_grad.T
    step = 256
    for start in range(0, depth, step):
        found = None
        for bits, piece in enumerate(tokens):
            term = product(turned[:, bits * size : (bits + 1) * size], piece[:, start : start + step])
            found = term if found is None else found + term
        partial[start : start + step] = found.T
    chunk = kept_ref.shape[1]
    for out, side in ((kept_ref, half), (sent_ref, 1 - half)):
        for index in range(rows):
            out[index] = partial[at_offset(side * rows + index, chunk)].astype(out.dtype)


def spread(at, tokens, own_grad, arrived, earlier, rows, waits, through):
    size, depth = tokens[0].shape
    cols = own_grad.shape[1]
    chunk = depth // 2 // rows
    shape = (rows, chunk, cols)
    width = cols + (earlier[0].shape[1] if earlier else 0)
    piece = jax.ShapeDtypeStruct((size, width), jnp.bfloat16)
    outs = small_call(
        functools.partial(spread_kernel, rows=rows, before=len(earlier)),
        "spread", at, (*tokens, own_grad, arrived, *earlier),
        [
            piece,
            piece,
            jax.ShapeDtypeStruct((2, size, width), jnp.bfloat16),
            jax.ShapeDtypeStruct(shape, jnp.float32),
            jax.ShapeDtypeStruct(shape, jnp.bfloat16),
        ],
        [pltpu.VMEM((cols, LANES * size), jnp.bfloat16), pltpu.VMEM((depth, cols), jnp.float32)],
        waits=waits,
        through=through,
        cost=0,
    )
    return outs[:3], outs[3], outs[4], outs[5:]


def feature_kernel(at_ref, *refs, heads, counts):
    (own, beside, across), weights, (out_ref, tokens) = refs[:3], refs[3:-2], refs[-2:]
    pieces = (own, beside.at[0], across.at[0], across.at[1])
    step = pl.program_id(0)
    width = tokens.shape[1] // 2

    @pl.when(step == 0)
    def _():
        for head in range(heads):
            for bits in range(LANES):
                piece = pieces[bits][:, 2 * head * HEAD_DIM : 2 * (head + 1) * HEAD_DIM]
                column = (at_ref[0] ^ bits) * heads + head
                tokens[:, at_offset(column, HEAD_DIM)] = piece[:, :HEAD_DIM]
                tokens[:, at_offset(column + width // HEAD_DIM, HEAD_DIM)] = piece[:, HEAD_DIM:]

    first = 0
    for weight, count in zip(weights, counts):

        @pl.when((step >= first) & (step < first + count))
        def _(weight=weight):
            out_ref[0] = product_minor(tokens[...], weight[...]).astype(jnp.bfloat16)

        first += count


def feature_grads(at, found, weights, waits):
    pieces = found
    size = pieces[0].shape[0]
    heads = pieces[0].shape[1] // (2 * HEAD_DIM)
    step = 512
    counts = [weight.shape[0] // step for weight in weights]
    depth = sum(counts) * step
    starts = [sum(counts[:index]) for index in range(len(counts))]
    side, part = counts[0], counts[1]

    def place(index, at_ref):
        half, core = at_ref[1], at_ref[2]
        other = (1 - half) * side
        fetched = other + core * part + index - starts[1]
        passed = other + (1 - core) * part + index - starts[2]
        return jnp.where(
            index < starts[1],
            half * side + index,
            jnp.where(index < starts[2], fetched, passed),
        )

    def weight_spec(weight, start, count):
        return pl.BlockSpec(
            (step, weight.shape[1]), lambda index, _: (jnp.clip(index - start, 0, count - 1), 0)
        )

    return pl.pallas_call(
        ordered(
            functools.partial(feature_kernel, heads=heads, counts=counts),
            len(pieces) + len(weights),
            len(waits),
            1,
            0,
        ),
        grid_spec=pltpu.PrefetchScalarGridSpec(
            num_scalar_prefetch=1,
            grid=(sum(counts),),
            in_specs=[whole_block(piece) for piece in pieces]
            + [weight_spec(*found) for found in zip(weights, starts, counts)]
            + [pl.BlockSpec(memory_space=pl.ANY)] * len(waits),
            out_specs=pl.BlockSpec((1, size, step), lambda index, at_ref: (0, 0, place(index, at_ref))),
            scratch_shapes=[pltpu.VMEM((size, weights[0].shape[1]), jnp.bfloat16)],
        ),
        out_shape=jax.ShapeDtypeStruct((1, size, depth), jnp.bfloat16),
        compiler_params=pltpu.CompilerParams(vmem_limit_bytes=VMEM_GRANT),
        cost_estimate=time_estimate(6),
        name="feature_grads",
    )(at, *pieces, *weights, *waits)


def place_weight_kernel(at_ref, *refs, heads):
    *pieces, out = refs
    width = out.shape[1] // 2
    for bits, piece in enumerate(pieces):
        for head in range(heads):
            column = (at_ref[0] ^ bits) * heads + head
            start = 2 * head * HEAD_DIM
            out[:, at_offset(column, HEAD_DIM)] = piece[:, start : start + HEAD_DIM]
            out[:, at_offset(column + width // HEAD_DIM, HEAD_DIM)] = piece[
                :, start + HEAD_DIM : start + 2 * HEAD_DIM
            ]


def place_weight(at, pieces, waits):
    count, cols = pieces[0].shape
    whole = jax.ShapeDtypeStruct((count, LANES * cols), jnp.float32)
    return small_call(
        functools.partial(place_weight_kernel, heads=cols // (2 * HEAD_DIM)),
        "place_weight", at, pieces, [whole], waits=waits,
    )[0]


def merge_kernel(at_ref, *refs, place):
    *inputs, kept_ref, sent_ref = refs
    bit = at_ref[place]
    for index in range(kept_ref.shape[0]):
        for out, high in ((kept_ref, bit), (sent_ref, 1 - bit)):
            found = inputs[0][2 * index + high]
            for arrived in inputs[1:]:
                found = found + arrived[2 * index + high].astype(jnp.float32)
            out[index] = found.astype(out.dtype)


def merge(at, place, kept, arrived, waits=()):
    shape = (kept.shape[0] // 2, *kept.shape[1:])
    return small_call(
        functools.partial(merge_kernel, place=place),
        "merge", at, (kept, *arrived),
        [jax.ShapeDtypeStruct(shape, jnp.float32), jax.ShapeDtypeStruct(shape, jnp.bfloat16)],
        waits=waits,
    )


def finish_kernel(at_ref, *refs, heads, each):
    inputs, outs = refs[: heads * each], refs[heads * each : -1]
    total = refs[-1]
    size = outs[0].shape[0]
    cols = inputs[0].shape[2]
    for head in range(heads):
        found = inputs[head * each][0]
        for arrived in inputs[head * each + 1 : (head + 1) * each]:
            found = found + arrived[0].astype(jnp.float32)
        total[:, head * cols : (head + 1) * cols] = found
    for bits, out in enumerate(outs):
        out[...] = total[at_offset(at_ref[0] ^ bits, size)]


def finish(at, parts, waits):
    _, chunk, cols = parts[0][0].shape
    heads = len(parts)
    piece = jax.ShapeDtypeStruct((chunk // LANES, heads * cols), jnp.float32)
    return small_call(
        functools.partial(finish_kernel, heads=heads, each=len(parts[0])),
        "finish", at, [value for part in parts for value in part], [piece] * LANES,
        [pltpu.VMEM((chunk, heads * cols), jnp.float32)],
        waits=waits,
    )


def passed_round(pieces):
    return [exchanged(piece, bits) if bits else piece for bits, piece in enumerate(pieces)]


def local(features, queries, kv_weight, upstream):
    tokens = features[0]
    size = tokens.shape[0]
    weight_rows, kv_width = kv_weight.shape
    width = kv_width // 2
    lane_width = width // LANES
    heads = lane_width // HEAD_DIM
    rows = lax.axis_size("seq") // LANES
    place = lax.axis_index("seq")
    lane = place % LANES
    row = place // LANES
    half = lax.axis_index("dp")
    core = place % 2

    here = jnp.stack([lane, half]).astype(jnp.int32)
    dealt = deal_heads(here, queries, upstream)
    lane_weight = take_columns(here, kv_weight, dealt[0][:1])
    other_lane_weight = swapped(lane_weight)
    across = exchanged(tokens, 2)
    beside = exchanged(tokens, 1)
    diagonal = exchanged(across, 1)
    row_tokens = (tokens, beside, across, diagonal)

    owns = project(here, row_tokens, (lane_weight, other_lane_weight))
    windows = [(own, shifted(own, 1)) for own in owns]

    part_rows = weight_rows // 2
    through = [lax.dynamic_slice_in_dim(kv_weight, core * part_rows, part_rows, 0)]
    own_pairs = []
    for pieces in dealt:
        own_pair, *handed = place_rows(here, go_round(here, pieces), owns[:1], through)
        if through:
            (part,) = handed
        through = []
        own_pairs.append(own_pair)
    next_pairs = [shifted(own_pair, -1) for own_pair in own_pairs]

    fetched = swapped(part)

    at = jnp.stack([row, lane]).astype(jnp.int32)
    shared = []
    for head in range(heads):
        own_stats, next_stats = softmax_stats(
            at, own_pairs[head], next_pairs[head], windows[head], size
        )
        shared.append(
            (own_stats, turned_round(next_stats, 1), next_stats, turned_round(own_stats, -1))
        )
    gained = [
        attention_grads(
            at, own_pairs[head], next_pairs[head], windows[head], shared[head], size,
            (shared[-1][0],),
        )
        for head in range(heads)
    ]

    bits = jnp.stack([(row >> index) % 2 for index in range(rows.bit_length() - 1)])
    kv_pieces, parts, out_pieces = [], [], []
    waits, through = (gained[-1][3],), (fetched,)
    for head, (own_out, next_out, near_grad, own_grad) in enumerate(gained):
        if head:
            through = (next_out,)
        else:
            next_out = shifted(next_out, 1)
        kv_pieces, kept, sent, (handed,) = spread(
            here, row_tokens, own_grad, shifted(near_grad, -1), kv_pieces, rows, waits, through
        )
        if head:
            next_out = shifted(handed, 1)
        else:
            fetched = handed
            passed = exchanged(fetched, 1)
        out_pieces.append(go_round(here, settle_out(here, own_out, next_out, (sent,))))
        arrived = [swapped(sent)]
        waits = ()
        distance = 1
        while distance < rows:
            kept, sent = merge(bits, distance.bit_length() - 1, kept, arrived)
            arrived = [moved(sent, distance * LANES, 0)]
            if not waits:
                waits = (sent,)
            distance *= 2
        parts.append((kept, *arrived))
    kv_found = go_round(here, kv_pieces)

    feature_grad = feature_grads(
        jnp.stack([lane, half, core]).astype(jnp.int32),
        kv_found,
        (kv_weight, fetched, passed),
        (sent,),
    )
    attended, query_grad = place_heads(here, out_pieces)
    pieces = passed_round(finish(here, parts, (feature_grad,)))
    weight_grad = place_weight(here, pieces, (attended,))
    return (attended, query_grad, feature_grad, weight_grad)


def solution(mesh):
    return jax.shard_map(
        local,
        mesh=mesh,
        in_specs=(P("dp", "seq", None), P("dp", "seq", None), P("dp", None), P("dp", "seq", None)),
        out_specs=(
            P("dp", "seq", None),
            P("dp", "seq", None),
            P("dp", "seq", None),
            P(("dp", "seq"), None),
        ),
        check_vma=False,
    )
```

```python
import functools
import math

import jax
import jax.numpy as jnp
from jax import lax
from jax.experimental import pallas as pl
from jax.experimental.pallas import tpu as pltpu
from jax.sharding import PartitionSpec as P

HEAD_DIM = 128
WINDOW = 2048
LANES = 4
VMEM_GRANT = 24 * 2**20
SCORE_SCALE = 1.0 / math.sqrt(HEAD_DIM)
EXP2_SCALE = SCORE_SCALE * math.log2(math.e)
MASKED = -1e30
MINOR_DIMS = (((1,), (1,)), ((), ()))
MAJOR_DIMS = (((0,), (0,)), ((), ()))


def exchanged(value, bits):
    count = lax.axis_size("seq")
    return lax.ppermute(value, "seq", [(source, source ^ bits) for source in range(count)])


def shifted(value, rows):
    count = lax.axis_size("seq")
    steps = rows * LANES
    leading, last = (max(0, -steps), min(count, count - steps))
    return lax.ppermute(value, "seq", [(source, source + steps) for source in range(leading, last)])


def turned_round(value, rows):
    count = lax.axis_size("seq")
    pairs = [(source, (source + rows * LANES) % count) for source in range(count)]
    return lax.ppermute(value, "seq", pairs)


def moved(value, bits, across):
    count = lax.axis_size("seq")
    pairs = [
        (2 * place + side, 2 * (place ^ bits) + (side ^ across))
        for place in range(count)
        for side in range(2)
    ]
    return lax.ppermute(value, ("seq", "dp"), pairs)


def swapped(value):
    return lax.ppermute(value, "dp", [(0, 1), (1, 0)])


def by_sublane(block, reduce):
    return reduce(block.reshape(block.shape[0] // 8, 8, block.shape[1]), axis=0)


def product(left, right):
    return jnp.dot(left, right, preferred_element_type=jnp.float32)


def product_minor(left, right):
    return lax.dot_general(left, right, MINOR_DIMS, preferred_element_type=jnp.float32)


def project_kernel(at_ref, *refs, heads):
    tokens, here_ref, there_ref, outs = refs[:LANES], refs[LANES], refs[LANES + 1], refs[-heads:]
    lane, half = at_ref[0], at_ref[1]
    depth = here_ref.shape[0]
    for bits, piece in enumerate(tokens):
        here = piece[:, at_offset(half, depth)]
        there = piece[:, at_offset(1 - half, depth)]
        whole = product(here, here_ref[...]) + product(there, there_ref[...])
        held = at_offset(lane ^ bits, piece.shape[0])
        width = whole.shape[1] // heads
        for head, out in enumerate(outs):
            out[held] = whole[:, head * width : (head + 1) * width].astype(jnp.bfloat16)


def project(at, tokens, weights):
    heads = weights[0].shape[1] // (2 * HEAD_DIM)
    whole = jax.ShapeDtypeStruct((LANES * tokens[0].shape[0], 2 * HEAD_DIM), jnp.bfloat16)
    return small_call(
        functools.partial(project_kernel, heads=heads),
        "project", at, (*tokens, *weights), [whole] * heads, cost=4,
    )


def visits(blocks):
    for turn in range(blocks):
        whole = [(1, lane, None) for lane in range(blocks)]
        yield 0, turn, whole + [(0, lane, "low" if lane == turn else None) for lane in range(turn + 1)]
        yield 1, turn, [(1, lane, "high" if lane == turn else None) for lane in range(turn, blocks)]


def masked(score, near, edge, near_bias):
    if edge:
        key_pos = lax.broadcasted_iota(jnp.int32, score.shape, 0)
        query_pos = lax.broadcasted_iota(jnp.int32, score.shape, 1)
        allowed = key_pos <= query_pos if edge == "low" else key_pos > query_pos
        score = jnp.where(allowed, score, MASKED)
    return score + near_bias if near else score


def stats_kernel(
    at_ref, own_pair, next_pair, own_ref, near_ref, own_out, next_out, scores, *, blocks, size
):
    near_bias = jnp.where(at_ref[0] > 0, 0.0, MASKED)
    window = (own_ref, near_ref)
    pairs = (own_pair, next_pair)
    outs = (own_out, next_out)
    for turn, (side, block, keys) in enumerate(visits(blocks)):
        held = slice(block * size, (block + 1) * size)
        peak = jnp.full((8, size), MASKED, jnp.float32)
        for index, (near, lane, edge) in enumerate(keys):
            key = window[near][lane * size : (lane + 1) * size, :HEAD_DIM]
            score = masked(product_minor(key, pairs[side][0, held]), near, edge, near_bias)
            scores[turn % 2, index] = score
            peak = jnp.maximum(peak, by_sublane(score, jnp.max))
        peak = jnp.max(peak, axis=0, keepdims=True)
        mass = jnp.zeros((8, size), jnp.float32)
        pull = jnp.zeros((8, size), jnp.float32)
        for index, (near, lane, edge) in enumerate(keys):
            value = window[near][lane * size : (lane + 1) * size, HEAD_DIM:]
            grown = jnp.exp2((scores[turn % 2, index] - peak) * EXP2_SCALE)
            mass = mass + by_sublane(grown, jnp.sum)
            pull = pull + by_sublane(grown * product_minor(value, pairs[side][1, held]), jnp.sum)
        out = outs[side]
        out[0:1, held] = peak
        out[1:2, held] = jnp.sum(mass, axis=0, keepdims=True)
        out[2:3, held] = jnp.sum(pull, axis=0, keepdims=True)
        out[3:, held] = jnp.zeros((5, size), jnp.float32)


def settled(here, there, there_valid):
    here_peak = here[0:1]
    there_peak = jnp.where(there_valid, there[0:1], MASKED)
    peak = jnp.maximum(here_peak, there_peak)
    here_factor = jnp.exp2((here_peak - peak) * EXP2_SCALE)
    there_factor = jnp.exp2((there_peak - peak) * EXP2_SCALE)
    mass = here[1:2] * here_factor + there[1:2] * there_factor
    pull = here[2:3] * here_factor + there[2:3] * there_factor
    share = jnp.where(mass > 0, 1.0 / mass, 0.0)
    return peak, share, pull * share


def gradient_kernel(
    at_ref, own_pair, next_pair, own_ref, near_ref,
    own_stats, far_stats, next_stats, main_stats, *refs, blocks, size,
):
    *earlier, own_out, next_out, near_grad, own_grad = refs[:-7]
    turned, queries, cotangents, own_weights, own_dscores, near_weights, near_dscores = refs[-7:]
    joined = next_out.shape[2] - HEAD_DIM
    if earlier:
        next_out[:, :, :joined] = earlier[0][...]
    near_valid = at_ref[0] > 0
    near_bias = jnp.where(near_valid, 0.0, MASKED)
    window = (own_ref, near_ref)
    row_tokens = blocks * size
    pairs = (own_pair, next_pair)
    outs = (own_out, next_out.at[:, :, joined:])
    weights = (own_weights, near_weights)
    dscores = (own_dscores, near_dscores)
    figures = (
        settled(own_stats[...], far_stats[...], near_valid),
        settled(next_stats[...], main_stats[...], True),
    )
    for side in range(2):
        queries[side * row_tokens : (side + 1) * row_tokens] = pairs[side][0]
        cotangents[side * row_tokens : (side + 1) * row_tokens] = pairs[side][1]
        for block in range(blocks):
            held = slice(block * size, (block + 1) * size)
            turned[side, :, held] = window[side][held].T
    for side, block, keys in visits(blocks):
        held = slice(block * size, (block + 1) * size)
        column = slice(side * row_tokens + block * size, side * row_tokens + (block + 1) * size)
        peak, share, centre = (figure[:, held] for figure in figures[side])
        scaled = share * SCORE_SCALE
        for near, lane, edge in keys:
            rows = slice(lane * size, (lane + 1) * size)
            score = product_minor(window[near][rows, :HEAD_DIM], pairs[side][0, held])
            dprob = product_minor(window[near][rows, HEAD_DIM:], pairs[side][1, held])
            grown = jnp.exp2((masked(score, near, edge, near_bias) - peak) * EXP2_SCALE)
            weights[near][rows, column] = (grown * share).astype(jnp.bfloat16)
            dscores[near][rows, column] = (grown * ((dprob - centre) * scaled)).astype(jnp.bfloat16)
        rows = slice(block * size if side else 0, row_tokens)
        attended = product(turned[1, HEAD_DIM:, rows], near_weights[rows, column])
        query_grad = product(turned[1, :HEAD_DIM, rows], near_dscores[rows, column])
        if not side:
            rows = slice(0, (block + 1) * size)
            attended += product(turned[0, HEAD_DIM:, rows], own_weights[rows, column])
            query_grad += product(turned[0, :HEAD_DIM, rows], own_dscores[rows, column])
        outs[side][0, held] = attended.T.astype(outs[side].dtype)
        outs[side][1, held] = query_grad.T.astype(outs[side].dtype)
    for lane in range(blocks):
        rows = slice(lane * size, (lane + 1) * size)
        met = slice(0, row_tokens + (lane + 1) * size)
        near_grad[rows, :HEAD_DIM] = product(near_dscores[rows, met], queries[met]).astype(
            jnp.bfloat16
        )
        near_grad[rows, HEAD_DIM:] = product(near_weights[rows, met], cotangents[met]).astype(
            jnp.bfloat16
        )
        met = slice(lane * size, row_tokens)
        own_grad[rows, :HEAD_DIM] = product(own_dscores[rows, met], queries[met])
        own_grad[rows, HEAD_DIM:] = product(own_weights[rows, met], cotangents[met])


def kernel_call(kernel, name, at, own_pair, next_pair, kvs, stats, out_shape, scratch, size, waits, cost, grant):
    row_tokens = own_pair.shape[1]
    blocks = row_tokens // size

    return pl.pallas_call(
        ordered(
            functools.partial(kernel, blocks=blocks, size=size),
            2 + len(kvs) + len(stats),
            len(waits),
            len(out_shape),
            0,
        ),
        grid_spec=pltpu.PrefetchScalarGridSpec(
            num_scalar_prefetch=1,
            grid=(1,),
            in_specs=[whole_block(value) for value in (own_pair, next_pair, *kvs, *stats)]
            + [pl.BlockSpec(memory_space=pl.ANY)] * len(waits),
            out_specs=[whole_block(value) for value in out_shape],
            scratch_shapes=scratch,
        ),
        out_shape=out_shape,
        compiler_params=pltpu.CompilerParams(vmem_limit_bytes=grant),
        cost_estimate=time_estimate(cost),
        name=name,
    )(at, own_pair, next_pair, *kvs, *stats, *waits)


def softmax_stats(at, own_pair, next_pair, kvs, size):
    row_tokens = own_pair.shape[1]
    return kernel_call(
        stats_kernel, "softmax_stats", at, own_pair, next_pair, kvs, (),
        [jax.ShapeDtypeStruct((8, row_tokens), jnp.float32)] * 2,
        [pltpu.VMEM((2, 2 * row_tokens // size, size, size), jnp.float32)],
        size, (), 4, 20 * 2**20,
    )


def attention_grads(at, own_pair, next_pair, kvs, stats, earlier, size, waits):
    row_tokens = own_pair.shape[1]
    low = jnp.bfloat16
    width = HEAD_DIM + (earlier[0].shape[2] if earlier else 0)
    return kernel_call(
        gradient_kernel, "attention_grads", at, own_pair, next_pair, kvs, (*stats, *earlier),
        [
            jax.ShapeDtypeStruct((2, row_tokens, HEAD_DIM), jnp.float32),
            jax.ShapeDtypeStruct((2, row_tokens, width), low),
            jax.ShapeDtypeStruct((row_tokens, 2 * HEAD_DIM), low),
            jax.ShapeDtypeStruct((row_tokens, 2 * HEAD_DIM), jnp.float32),
        ],
        [
            pltpu.VMEM((2, 2 * HEAD_DIM, row_tokens), low),
            pltpu.VMEM((2 * row_tokens, HEAD_DIM), low),
            pltpu.VMEM((2 * row_tokens, HEAD_DIM), low),
            pltpu.VMEM((row_tokens, row_tokens), low),
            pltpu.VMEM((row_tokens, row_tokens), low),
            pltpu.VMEM((row_tokens, 2 * row_tokens), low),
            pltpu.VMEM((row_tokens, 2 * row_tokens), low),
        ],
        size, waits, 8, 40 * 2**20,
    )


def at_offset(index, size):
    return pl.ds(pl.multiple_of(index * size, size), size)


def ordered(kernel, inputs, waits, outputs, through):
    def body(*refs):
        first = 1 + inputs + waits + through
        kept = first + outputs
        return kernel(*refs[: 1 + inputs], *refs[first:kept], *refs[kept + through :])

    return body


def time_estimate(microseconds):
    return pl.CostEstimate(
        flops=microseconds * 10**9, bytes_accessed=microseconds * 3 * 10**6, transcendentals=0
    )


def work_estimate(microseconds):
    return pl.CostEstimate(flops=microseconds * 10**9, bytes_accessed=0, transcendentals=0)


def whole_block(value):
    return pl.BlockSpec(value.shape, lambda *_: (0,) * len(value.shape))


def small_call(
    kernel, name, at, operands, out_shape, scratch=(), waits=(), through=(), cost=1
):
    anywhere = pl.BlockSpec(memory_space=pl.ANY)
    first = 1 + len(operands) + len(waits)
    return pl.pallas_call(
        ordered(kernel, len(operands), len(waits), len(out_shape), len(through)),
        grid=(1,),
        in_specs=[pl.BlockSpec(memory_space=pltpu.SMEM)]
        + [whole_block(value) for value in operands]
        + [anywhere] * len(waits)
        + [pl.BlockSpec(memory_space=pltpu.HBM)] * len(through),
        out_specs=[whole_block(value) for value in out_shape]
        + [pl.BlockSpec(memory_space=pltpu.HBM)] * len(through),
        out_shape=[
            *out_shape,
            *(jax.ShapeDtypeStruct(value.shape, value.dtype) for value in through),
        ],
        input_output_aliases={
            first + index: len(out_shape) + index for index in range(len(through))
        },
        scratch_shapes=list(scratch),
        compiler_params=pltpu.CompilerParams(vmem_limit_bytes=VMEM_GRANT),
        cost_estimate=time_estimate(cost),
        name=name,
    )(at, *operands, *waits, *through)


def mixed_kernel(_, held_ref, passed_ref, out):
    out[0] = held_ref[...]
    out[1] = passed_ref[1]


def go_round(at, pieces):
    own, held, given = pieces
    beside = exchanged(given, 1)
    shape = jax.ShapeDtypeStruct(given.shape, given.dtype)
    (both,) = small_call(mixed_kernel, "mix", at, (held, beside), [shape])
    across = exchanged(both, 2)
    return own, beside, across


def deal_kernel(at_ref, query_ref, cotangent_ref, *refs):
    columns, outs, taken_ref = refs[: -LANES - 1], refs[-LANES - 1 : -1], refs[-1]
    width = outs[0].shape[2]
    for bits, out in enumerate(outs):
        held = at_offset(at_ref[0] ^ bits, width)
        out[0] = query_ref[0, :, held]
        out[1] = cotangent_ref[0, :, held]
    for index, column in enumerate(columns):
        taken_ref[:, index * HEAD_DIM : (index + 1) * HEAD_DIM] = column[...]


def deal(at, queries, upstream, weight):
    _, size, width = queries.shape
    depth = weight.shape[0]
    heads = width // LANES // HEAD_DIM
    piece = jax.ShapeDtypeStruct((2, size, width // LANES), jnp.bfloat16)
    taken = jax.ShapeDtypeStruct((depth, 2 * heads * HEAD_DIM), weight.dtype)

    def column(index):
        first = index % 2 * (width // HEAD_DIM) + index // 2
        return pl.BlockSpec((depth, HEAD_DIM), lambda _, at_ref: (0, first + at_ref[0] * heads))

    outs = pl.pallas_call(
        deal_kernel,
        grid_spec=pltpu.PrefetchScalarGridSpec(
            num_scalar_prefetch=1,
            grid=(1,),
            in_specs=[whole_block(queries), whole_block(upstream)]
            + [column(index) for index in range(2 * heads)],
            out_specs=[whole_block(piece)] * LANES + [whole_block(taken)],
        ),
        out_shape=[piece] * LANES + [taken],
        compiler_params=pltpu.CompilerParams(vmem_limit_bytes=VMEM_GRANT),
        cost_estimate=work_estimate(2),
        name="deal",
    )(at, queries, upstream, *[weight] * (2 * heads))
    return outs[:LANES], outs[LANES]


def take_rows_kernel(_, weight_ref, out_ref):
    out_ref[...] = weight_ref[...]


def take_rows(at, weight):
    shape = (weight.shape[0] // 2, weight.shape[1])
    return pl.pallas_call(
        take_rows_kernel,
        grid_spec=pltpu.PrefetchScalarGridSpec(
            num_scalar_prefetch=1,
            grid=(1,),
            in_specs=[pl.BlockSpec(shape, lambda _, at_ref: (at_ref[2], 0))],
            out_specs=pl.BlockSpec(shape, lambda *_: (0, 0)),
        ),
        out_shape=jax.ShapeDtypeStruct(shape, weight.dtype),
        compiler_params=pltpu.CompilerParams(vmem_limit_bytes=VMEM_GRANT),
        cost_estimate=work_estimate(2),
        name="take_rows",
    )(at, weight)


def place_rows_kernel(at_ref, *refs):
    pieces, outs = refs[:LANES], refs[LANES:]
    size = pieces[0].shape[1]
    for bits, piece in enumerate(pieces):
        for head, out in enumerate(outs):
            column = slice(head * HEAD_DIM, (head + 1) * HEAD_DIM)
            out[:, at_offset(at_ref[0] ^ bits, size)] = piece[:, :, column]


def place_rows(at, pieces, waits, through):
    kinds, size, width = pieces[0].shape
    heads = width // HEAD_DIM
    whole = jax.ShapeDtypeStruct((kinds, LANES * size, HEAD_DIM), pieces[0].dtype)
    outs = small_call(
        place_rows_kernel, "place_rows", at, pieces, [whole] * heads, waits=waits, through=through
    )
    return outs[:heads], outs[heads:]


TOKEN = jax.ShapeDtypeStruct((8, 128), jnp.float32)


def settle_kernel(at_ref, *refs, heads):
    own_outs, arrived, (own, held, given) = refs[:heads], refs[heads], refs[heads + 1 :]
    size = own.shape[1]
    for bits, out in enumerate((own, given.at[0], held, given.at[1])):
        rows = at_offset(at_ref[0] ^ bits, size)
        for head, own_out in enumerate(own_outs):
            column = slice(head * HEAD_DIM, (head + 1) * HEAD_DIM)
            whole = own_out[:, rows] + arrived[:, rows, column].astype(jnp.float32)
            out[:, :, column] = whole.astype(jnp.bfloat16)


def settle_outs(at, own_outs, arrived, waits):
    kinds, count, width = arrived.shape
    piece = jax.ShapeDtypeStruct((kinds, count // LANES, width), jnp.bfloat16)
    pair = jax.ShapeDtypeStruct((2, *piece.shape), jnp.bfloat16)
    return small_call(
        functools.partial(settle_kernel, heads=len(own_outs)),
        "settle_outs", at, (*own_outs, arrived), [piece, piece, pair], waits=waits,
    )


def place_heads_kernel(at_ref, own, beside, across, *outs):
    *outs, token = outs
    token[...] = jnp.zeros_like(token)
    width = own.shape[2]
    for bits, piece in enumerate((own, beside.at[0], across.at[0], across.at[1])):
        column = at_offset(at_ref[0] ^ bits, width)
        for kind, out in enumerate(outs):
            out[0, :, column] = piece[kind]


def place_heads(at, found):
    kinds, size, width = found[0].shape
    whole = jax.ShapeDtypeStruct((1, size, LANES * width), jnp.bfloat16)
    return small_call(place_heads_kernel, "place_heads", at, found, [whole] * kinds + [TOKEN])


def spread_kernel(at_ref, *refs, rows, before):
    tokens, own_ref, arrived_ref = refs[:LANES], refs[LANES], refs[LANES + 1]
    earlier = refs[LANES + 2 : LANES + 2 + before]
    own, held, given, kept_ref, sent_ref = refs[LANES + 2 + before : -2]
    kv_pieces = (own, given.at[0], held, given.at[1])
    if before:
        earlier = (earlier[0], earlier[2].at[0], earlier[1], earlier[2].at[1])
    turned, partial = refs[-2:]
    lane, half = at_ref[0], at_ref[1]
    size, depth = tokens[0].shape
    cols = own_ref.shape[1]
    for bits, piece in enumerate(kv_pieces):
        held = at_offset(lane ^ bits, size)
        kv_grad = (own_ref[held] + arrived_ref[held].astype(jnp.float32)).astype(jnp.bfloat16)
        if before:
            piece[:, : own.shape[1] - cols] = earlier[bits][...]
        piece[:, own.shape[1] - cols :] = kv_grad
        turned[:, bits * size : (bits + 1) * size] = kv_grad.T
    step = 256
    for start in range(0, depth, step):
        found = None
        for bits, piece in enumerate(tokens):
            term = product(turned[:, bits * size : (bits + 1) * size], piece[:, start : start + step])
            found = term if found is None else found + term
        partial[start : start + step] = found.T
    chunk = kept_ref.shape[1]
    for out, side in ((kept_ref, half), (sent_ref, 1 - half)):
        for index in range(rows):
            out[index] = partial[at_offset(side * rows + index, chunk)].astype(out.dtype)


def spread(at, tokens, own_grad, arrived, earlier, rows, waits, through):
    size, depth = tokens[0].shape
    cols = own_grad.shape[1]
    chunk = depth // 2 // rows
    shape = (rows, chunk, cols)
    width = cols + (earlier[0].shape[1] if earlier else 0)
    piece = jax.ShapeDtypeStruct((size, width), jnp.bfloat16)
    outs = small_call(
        functools.partial(spread_kernel, rows=rows, before=len(earlier)),
        "spread", at, (*tokens, own_grad, arrived, *earlier),
        [
            piece,
            piece,
            jax.ShapeDtypeStruct((2, size, width), jnp.bfloat16),
            jax.ShapeDtypeStruct(shape, jnp.float32),
            jax.ShapeDtypeStruct(shape, jnp.bfloat16),
        ],
        [pltpu.VMEM((cols, LANES * size), jnp.bfloat16), pltpu.VMEM((depth, cols), jnp.float32)],
        waits=waits,
        through=through,
        cost=0,
    )
    return outs[:3], outs[3], outs[4], outs[5:]


def feature_kernel(at_ref, *refs, heads, counts):
    (own, beside, across), weights, (out_ref, token, tokens) = refs[:3], refs[3:-3], refs[-3:]
    pieces = (own, beside.at[0], across.at[0], across.at[1])
    step = pl.program_id(0)
    width = tokens.shape[1] // 2

    @pl.when(step == 0)
    def _():
        token[...] = jnp.zeros_like(token)
        for head in range(heads):
            for bits in range(LANES):
                piece = pieces[bits][:, 2 * head * HEAD_DIM : 2 * (head + 1) * HEAD_DIM]
                column = (at_ref[0] ^ bits) * heads + head
                tokens[:, at_offset(column, HEAD_DIM)] = piece[:, :HEAD_DIM]
                tokens[:, at_offset(column + width // HEAD_DIM, HEAD_DIM)] = piece[:, HEAD_DIM:]

    first = 0
    for weight, count in zip(weights, counts):

        @pl.when((step >= first) & (step < first + count))
        def _(weight=weight):
            out_ref[0] = product_minor(tokens[...], weight[...]).astype(jnp.bfloat16)

        first += count


def feature_grads(at, found, weights, waits):
    pieces = found
    size = pieces[0].shape[0]
    heads = pieces[0].shape[1] // (2 * HEAD_DIM)
    step = 512
    counts = [weight.shape[0] // step for weight in weights]
    depth = sum(counts) * step
    starts = [sum(counts[:index]) for index in range(len(counts))]
    side, part = counts[0], counts[1]

    def place(index, at_ref):
        half, core = at_ref[1], at_ref[2]
        other = (1 - half) * side
        fetched = other + core * part + index - starts[1]
        passed = other + (1 - core) * part + index - starts[2]
        return jnp.where(
            index < starts[1],
            half * side + index,
            jnp.where(index < starts[2], fetched, passed),
        )

    def weight_spec(weight, start, count):
        return pl.BlockSpec(
            (step, weight.shape[1]), lambda index, _: (jnp.clip(index - start, 0, count - 1), 0)
        )

    return pl.pallas_call(
        ordered(
            functools.partial(feature_kernel, heads=heads, counts=counts),
            len(pieces) + len(weights),
            len(waits),
            2,
            0,
        ),
        grid_spec=pltpu.PrefetchScalarGridSpec(
            num_scalar_prefetch=1,
            grid=(sum(counts),),
            in_specs=[whole_block(piece) for piece in pieces]
            + [weight_spec(*found) for found in zip(weights, starts, counts)]
            + [pl.BlockSpec(memory_space=pl.ANY)] * len(waits),
            out_specs=[
                pl.BlockSpec((1, size, step), lambda index, at_ref: (0, 0, place(index, at_ref))),
                whole_block(TOKEN),
            ],
            scratch_shapes=[pltpu.VMEM((size, weights[0].shape[1]), jnp.bfloat16)],
        ),
        out_shape=[jax.ShapeDtypeStruct((1, size, depth), jnp.bfloat16), TOKEN],
        compiler_params=pltpu.CompilerParams(vmem_limit_bytes=VMEM_GRANT),
        cost_estimate=time_estimate(6),
        name="feature_grads",
    )(at, *pieces, *weights, *waits)


def place_weight_kernel(at_ref, *refs, heads):
    *pieces, out = refs
    width = out.shape[1] // 2
    for bits, piece in enumerate(pieces):
        for head in range(heads):
            column = (at_ref[0] ^ bits) * heads + head
            start = 2 * head * HEAD_DIM
            out[:, at_offset(column, HEAD_DIM)] = piece[:, start : start + HEAD_DIM]
            out[:, at_offset(column + width // HEAD_DIM, HEAD_DIM)] = piece[
                :, start + HEAD_DIM : start + 2 * HEAD_DIM
            ]


def place_weight(at, pieces, waits):
    count, cols = pieces[0].shape
    whole = jax.ShapeDtypeStruct((count, LANES * cols), jnp.float32)
    return small_call(
        functools.partial(place_weight_kernel, heads=cols // (2 * HEAD_DIM)),
        "place_weight", at, pieces, [whole], waits=waits,
    )[0]


def merge_kernel(at_ref, *refs, place):
    *inputs, kept_ref, sent_ref = refs
    bit = at_ref[place]
    for index in range(kept_ref.shape[0]):
        for out, high in ((kept_ref, bit), (sent_ref, 1 - bit)):
            found = inputs[0][2 * index + high]
            for arrived in inputs[1:]:
                found = found + arrived[2 * index + high].astype(jnp.float32)
            out[index] = found.astype(out.dtype)


def merge(at, place, kept, arrived, waits=()):
    shape = (kept.shape[0] // 2, *kept.shape[1:])
    return small_call(
        functools.partial(merge_kernel, place=place),
        "merge", at, (kept, *arrived),
        [jax.ShapeDtypeStruct(shape, jnp.float32), jax.ShapeDtypeStruct(shape, jnp.bfloat16)],
        waits=waits,
    )


def finish_kernel(at_ref, *refs, heads, each):
    inputs, outs = refs[: heads * each], refs[heads * each : -1]
    total = refs[-1]
    size = outs[0].shape[0]
    cols = inputs[0].shape[2]
    for head in range(heads):
        found = inputs[head * each][0]
        for arrived in inputs[head * each + 1 : (head + 1) * each]:
            found = found + arrived[0].astype(jnp.float32)
        total[:, head * cols : (head + 1) * cols] = found
    for bits, out in enumerate(outs):
        out[...] = total[at_offset(at_ref[0] ^ bits, size)]


def finish(at, parts, waits):
    _, chunk, cols = parts[0][0].shape
    heads = len(parts)
    piece = jax.ShapeDtypeStruct((chunk // LANES, heads * cols), jnp.float32)
    return small_call(
        functools.partial(finish_kernel, heads=heads, each=len(parts[0])),
        "finish", at, [value for part in parts for value in part], [piece] * LANES,
        [pltpu.VMEM((chunk, heads * cols), jnp.float32)],
        waits=waits,
    )


def passed_round(pieces):
    return [exchanged(piece, bits) if bits else piece for bits, piece in enumerate(pieces)]


def local(features, queries, kv_weight, upstream):
    tokens = features[0]
    size = tokens.shape[0]
    weight_rows, kv_width = kv_weight.shape
    width = kv_width // 2
    lane_width = width // LANES
    heads = lane_width // HEAD_DIM
    rows = lax.axis_size("seq") // LANES
    place = lax.axis_index("seq")
    lane = place % LANES
    row = place // LANES
    half = lax.axis_index("dp")
    core = place % 2

    here = jnp.stack([lane, half, core]).astype(jnp.int32)
    pair_pieces, lane_weight = deal(here, queries, upstream, kv_weight)
    other_lane_weight = swapped(lane_weight)
    across = exchanged(tokens, 2)
    beside = exchanged(tokens, 1)
    diagonal = exchanged(across, 1)
    row_tokens = (tokens, beside, across, diagonal)

    owns = project(here, row_tokens, (lane_weight, other_lane_weight))
    windows = [(own, shifted(own, 1)) for own in owns]

    part = take_rows(here, kv_weight)
    own_pairs, (part,) = place_rows(here, passed_round(pair_pieces), owns[:1], (part,))
    next_pairs = [shifted(own_pair, -1) for own_pair in own_pairs]

    fetched = swapped(part)

    at = jnp.stack([row, lane]).astype(jnp.int32)
    shared = []
    for head in range(heads):
        own_stats, next_stats = softmax_stats(
            at, own_pairs[head], next_pairs[head], windows[head], size
        )
        shared.append(
            (own_stats, turned_round(next_stats, 1), next_stats, turned_round(own_stats, -1))
        )
    gained, next_out = [], ()
    for head in range(heads):
        gained.append(
            attention_grads(
                at, own_pairs[head], next_pairs[head], windows[head], shared[head], next_out, size,
                (shared[-1][0],),
            )
        )
        next_out = (gained[-1][1],)
    own_outs = [found[0] for found in gained]

    bits = jnp.stack([(row >> index) % 2 for index in range(rows.bit_length() - 1)])
    kv_pieces, parts = [], []
    waits, through = (gained[-1][3],), (fetched,)
    arrived_out = shifted(next_out[0], 1)
    for head, (_, _, near_grad, own_grad) in enumerate(gained):
        kv_pieces, kept, sent, handed = spread(
            here, row_tokens, own_grad, shifted(near_grad, -1), kv_pieces, rows, waits, through
        )
        if through:
            (fetched,) = handed
            passed = exchanged(fetched, 1)
        if head == heads - 1:
            kv_found = go_round(here, kv_pieces)
            out_found = go_round(here, settle_outs(here, own_outs, arrived_out, (sent,)))
        waits, through = (), ()
        arrived = [swapped(sent)]
        distance = 1
        while distance < rows:
            last = head == heads - 1 and 2 * distance == rows
            kept, sent = merge(
                bits, distance.bit_length() - 1, kept, arrived, kv_found[2:] if last else ()
            )
            arrived = [moved(sent, distance * LANES, 0)]
            if not waits:
                waits = (sent,)
            distance *= 2
        parts.append((kept, *arrived))

    feature_grad, feature_token = feature_grads(
        here,
        kv_found,
        (kv_weight, fetched, passed),
        (sent,),
    )
    attended, query_grad, token = place_heads(here, out_found)
    pieces = passed_round(finish(here, parts, (feature_token,)))
    weight_grad = place_weight(here, pieces, (token,))
    return (attended, query_grad, feature_grad, weight_grad)


def solution(mesh):
    return jax.shard_map(
        local,
        mesh=mesh,
        in_specs=(P("dp", "seq", None), P("dp", "seq", None), P("dp", None), P("dp", "seq", None)),
        out_specs=(
            P("dp", "seq", None),
            P("dp", "seq", None),
            P("dp", "seq", None),
            P(("dp", "seq"), None),
        ),
        check_vma=False,
    )
```

```python
import functools
import math

import jax
import jax.numpy as jnp
from jax import lax
from jax.experimental import pallas as pl
from jax.experimental.pallas import tpu as pltpu
from jax.sharding import PartitionSpec as P

HEAD_DIM = 128
WINDOW = 2048
LANES = 4
VMEM_GRANT = 24 * 2**20
SCORE_SCALE = 1.0 / math.sqrt(HEAD_DIM)
EXP2_SCALE = SCORE_SCALE * math.log2(math.e)
MASKED = -1e30
MINOR_DIMS = (((1,), (1,)), ((), ()))
MAJOR_DIMS = (((0,), (0,)), ((), ()))


def exchanged(value, bits):
    count = lax.axis_size("seq")
    return lax.ppermute(value, "seq", [(source, source ^ bits) for source in range(count)])


def shifted(value, rows):
    count = lax.axis_size("seq")
    steps = rows * LANES
    leading, last = (max(0, -steps), min(count, count - steps))
    return lax.ppermute(value, "seq", [(source, source + steps) for source in range(leading, last)])


def turned_round(value, rows):
    count = lax.axis_size("seq")
    pairs = [(source, (source + rows * LANES) % count) for source in range(count)]
    return lax.ppermute(value, "seq", pairs)


def moved(value, bits, across):
    count = lax.axis_size("seq")
    pairs = [
        (2 * place + side, 2 * (place ^ bits) + (side ^ across))
        for place in range(count)
        for side in range(2)
    ]
    return lax.ppermute(value, ("seq", "dp"), pairs)


def swapped(value):
    return lax.ppermute(value, "dp", [(0, 1), (1, 0)])


def by_sublane(block, reduce):
    return reduce(block.reshape(block.shape[0] // 8, 8, block.shape[1]), axis=0)


def product(left, right):
    return jnp.dot(left, right, preferred_element_type=jnp.float32)


def product_minor(left, right):
    return lax.dot_general(left, right, MINOR_DIMS, preferred_element_type=jnp.float32)


def project_kernel(at_ref, *refs, heads):
    tokens, here_ref, there_ref, outs = refs[:LANES], refs[LANES], refs[LANES + 1], refs[-heads:]
    lane, half = at_ref[0], at_ref[1]
    depth = here_ref.shape[0]
    for bits, piece in enumerate(tokens):
        here = piece[:, at_offset(half, depth)]
        there = piece[:, at_offset(1 - half, depth)]
        whole = product(here, here_ref[...]) + product(there, there_ref[...])
        held = at_offset(lane ^ bits, piece.shape[0])
        width = whole.shape[1] // heads
        for head, out in enumerate(outs):
            out[held] = whole[:, head * width : (head + 1) * width].astype(jnp.bfloat16)


def project(at, tokens, weights):
    heads = weights[0].shape[1] // (2 * HEAD_DIM)
    whole = jax.ShapeDtypeStruct((LANES * tokens[0].shape[0], 2 * HEAD_DIM), jnp.bfloat16)
    return small_call(
        functools.partial(project_kernel, heads=heads),
        "project", at, (*tokens, *weights), [whole] * heads, cost=4,
    )


def visits(blocks):
    for turn in range(blocks):
        whole = [(1, lane, None) for lane in range(blocks)]
        yield 0, turn, whole + [(0, lane, "low" if lane == turn else None) for lane in range(turn + 1)]
        yield 1, turn, [(1, lane, "high" if lane == turn else None) for lane in range(turn, blocks)]


def masked(score, near, edge, near_bias):
    if edge:
        key_pos = lax.broadcasted_iota(jnp.int32, score.shape, 0)
        query_pos = lax.broadcasted_iota(jnp.int32, score.shape, 1)
        allowed = key_pos <= query_pos if edge == "low" else key_pos > query_pos
        score = jnp.where(allowed, score, MASKED)
    return score + near_bias if near else score


def turn_kernel(_, near_ref, out_ref):
    size = out_ref.shape[0]
    for start in range(0, near_ref.shape[0], size):
        out_ref[:, start : start + size] = near_ref[start : start + size].T


def turned_over(at, near):
    shape = jax.ShapeDtypeStruct((near.shape[1], near.shape[0]), near.dtype)
    return small_call(turn_kernel, "turn", at, (near,), [shape])[0]


def stats_kernel(
    at_ref, own_pair, next_pair, own_ref, near_ref, own_out, next_out, scores, *, blocks, size
):
    near_bias = jnp.where(at_ref[0] > 0, 0.0, MASKED)
    window = (own_ref, near_ref)
    pairs = (own_pair, next_pair)
    outs = (own_out, next_out)
    for turn, (side, block, keys) in enumerate(visits(blocks)):
        held = slice(block * size, (block + 1) * size)
        peak = jnp.full((8, size), MASKED, jnp.float32)
        for index, (near, lane, edge) in enumerate(keys):
            key = window[near][lane * size : (lane + 1) * size, :HEAD_DIM]
            score = masked(product_minor(key, pairs[side][0, held]), near, edge, near_bias)
            scores[turn % 2, index] = score
            peak = jnp.maximum(peak, by_sublane(score, jnp.max))
        peak = jnp.max(peak, axis=0, keepdims=True)
        mass = jnp.zeros((8, size), jnp.float32)
        pull = jnp.zeros((8, size), jnp.float32)
        for index, (near, lane, edge) in enumerate(keys):
            value = window[near][lane * size : (lane + 1) * size, HEAD_DIM:]
            grown = jnp.exp2((scores[turn % 2, index] - peak) * EXP2_SCALE)
            mass = mass + by_sublane(grown, jnp.sum)
            pull = pull + by_sublane(grown * product_minor(value, pairs[side][1, held]), jnp.sum)
        out = outs[side]
        out[0:1, held] = peak
        out[1:2, held] = jnp.sum(mass, axis=0, keepdims=True)
        out[2:3, held] = jnp.sum(pull, axis=0, keepdims=True)
        out[3:, held] = jnp.zeros((5, size), jnp.float32)


def settled(here, there, there_valid):
    here_peak = here[0:1]
    there_peak = jnp.where(there_valid, there[0:1], MASKED)
    peak = jnp.maximum(here_peak, there_peak)
    here_factor = jnp.exp2((here_peak - peak) * EXP2_SCALE)
    there_factor = jnp.exp2((there_peak - peak) * EXP2_SCALE)
    mass = here[1:2] * here_factor + there[1:2] * there_factor
    pull = here[2:3] * here_factor + there[2:3] * there_factor
    share = jnp.where(mass > 0, 1.0 / mass, 0.0)
    return peak, share, pull * share


def gradient_kernel(
    at_ref, own_pair, next_pair, own_ref, near_ref, near_turned,
    own_stats, far_stats, next_stats, main_stats, *refs, blocks, size,
):
    *earlier, own_out, next_out, near_grad, own_grad = refs[:-7]
    own_turned, queries, cotangents, own_weights, own_dscores, near_weights, near_dscores = refs[-7:]
    turned = (own_turned, near_turned)
    joined = next_out.shape[2] - HEAD_DIM
    if earlier:
        next_out[:, :, :joined] = earlier[0][...]
    near_valid = at_ref[0] > 0
    near_bias = jnp.where(near_valid, 0.0, MASKED)
    window = (own_ref, near_ref)
    row_tokens = blocks * size
    pairs = (own_pair, next_pair)
    outs = (own_out, next_out.at[:, :, joined:])
    weights = (own_weights, near_weights)
    dscores = (own_dscores, near_dscores)
    figures = (
        settled(own_stats[...], far_stats[...], near_valid),
        settled(next_stats[...], main_stats[...], True),
    )
    for side in range(2):
        queries[side * row_tokens : (side + 1) * row_tokens] = pairs[side][0]
        cotangents[side * row_tokens : (side + 1) * row_tokens] = pairs[side][1]
    for block in range(blocks):
        held = slice(block * size, (block + 1) * size)
        own_turned[:, held] = own_ref[held].T
    for side, block, keys in visits(blocks):
        held = slice(block * size, (block + 1) * size)
        column = slice(side * row_tokens + block * size, side * row_tokens + (block + 1) * size)
        peak, share, centre = (figure[:, held] for figure in figures[side])
        scaled = share * SCORE_SCALE
        for near, lane, edge in keys:
            rows = slice(lane * size, (lane + 1) * size)
            score = product_minor(window[near][rows, :HEAD_DIM], pairs[side][0, held])
            dprob = product_minor(window[near][rows, HEAD_DIM:], pairs[side][1, held])
            grown = jnp.exp2((masked(score, near, edge, near_bias) - peak) * EXP2_SCALE)
            weights[near][rows, column] = (grown * share).astype(jnp.bfloat16)
            dscores[near][rows, column] = (grown * ((dprob - centre) * scaled)).astype(jnp.bfloat16)
        rows = slice(block * size if side else 0, row_tokens)
        attended = product(turned[1][HEAD_DIM:, rows], near_weights[rows, column])
        query_grad = product(turned[1][:HEAD_DIM, rows], near_dscores[rows, column])
        if not side:
            rows = slice(0, (block + 1) * size)
            attended += product(turned[0][HEAD_DIM:, rows], own_weights[rows, column])
            query_grad += product(turned[0][:HEAD_DIM, rows], own_dscores[rows, column])
        outs[side][0, held] = attended.T.astype(outs[side].dtype)
        outs[side][1, held] = query_grad.T.astype(outs[side].dtype)
    for lane in range(blocks):
        rows = slice(lane * size, (lane + 1) * size)
        met = slice(0, row_tokens + (lane + 1) * size)
        near_grad[rows, :HEAD_DIM] = product(near_dscores[rows, met], queries[met]).astype(
            jnp.bfloat16
        )
        near_grad[rows, HEAD_DIM:] = product(near_weights[rows, met], cotangents[met]).astype(
            jnp.bfloat16
        )
        met = slice(lane * size, row_tokens)
        own_grad[rows, :HEAD_DIM] = product(own_dscores[rows, met], queries[met])
        own_grad[rows, HEAD_DIM:] = product(own_weights[rows, met], cotangents[met])


def kernel_call(kernel, name, at, own_pair, next_pair, kvs, stats, out_shape, scratch, size, waits, cost, grant):
    row_tokens = own_pair.shape[1]
    blocks = row_tokens // size

    return pl.pallas_call(
        ordered(
            functools.partial(kernel, blocks=blocks, size=size),
            2 + len(kvs) + len(stats),
            len(waits),
            len(out_shape),
            0,
        ),
        grid_spec=pltpu.PrefetchScalarGridSpec(
            num_scalar_prefetch=1,
            grid=(1,),
            in_specs=[whole_block(value) for value in (own_pair, next_pair, *kvs, *stats)]
            + [pl.BlockSpec(memory_space=pl.ANY)] * len(waits),
            out_specs=[whole_block(value) for value in out_shape],
            scratch_shapes=scratch,
        ),
        out_shape=out_shape,
        compiler_params=pltpu.CompilerParams(vmem_limit_bytes=grant),
        cost_estimate=time_estimate(cost),
        name=name,
    )(at, own_pair, next_pair, *kvs, *stats, *waits)


def softmax_stats(at, own_pair, next_pair, kvs, size, waits):
    row_tokens = own_pair.shape[1]
    return kernel_call(
        stats_kernel, "softmax_stats", at, own_pair, next_pair, kvs, (),
        [jax.ShapeDtypeStruct((8, row_tokens), jnp.float32)] * 2,
        [pltpu.VMEM((2, 2 * row_tokens // size, size, size), jnp.float32)],
        size, waits, 4, 20 * 2**20,
    )


def attention_grads(at, own_pair, next_pair, kvs, stats, earlier, size, waits):
    row_tokens = own_pair.shape[1]
    low = jnp.bfloat16
    width = HEAD_DIM + (earlier[0].shape[2] if earlier else 0)
    return kernel_call(
        gradient_kernel, "attention_grads", at, own_pair, next_pair, kvs, (*stats, *earlier),
        [
            jax.ShapeDtypeStruct((2, row_tokens, HEAD_DIM), jnp.float32),
            jax.ShapeDtypeStruct((2, row_tokens, width), low),
            jax.ShapeDtypeStruct((row_tokens, 2 * HEAD_DIM), low),
            jax.ShapeDtypeStruct((row_tokens, 2 * HEAD_DIM), jnp.float32),
        ],
        [
            pltpu.VMEM((2 * HEAD_DIM, row_tokens), low),
            pltpu.VMEM((2 * row_tokens, HEAD_DIM), low),
            pltpu.VMEM((2 * row_tokens, HEAD_DIM), low),
            pltpu.VMEM((row_tokens, row_tokens), low),
            pltpu.VMEM((row_tokens, row_tokens), low),
            pltpu.VMEM((row_tokens, 2 * row_tokens), low),
            pltpu.VMEM((row_tokens, 2 * row_tokens), low),
        ],
        size, waits, 8, 40 * 2**20,
    )


def at_offset(index, size):
    return pl.ds(pl.multiple_of(index * size, size), size)


def ordered(kernel, inputs, waits, outputs, through):
    def body(*refs):
        first = 1 + inputs + waits + through
        kept = first + outputs
        return kernel(*refs[: 1 + inputs], *refs[first:kept], *refs[kept + through :])

    return body


def time_estimate(microseconds):
    return pl.CostEstimate(
        flops=microseconds * 10**9, bytes_accessed=microseconds * 3 * 10**6, transcendentals=0
    )


def work_estimate(microseconds):
    return pl.CostEstimate(flops=microseconds * 10**9, bytes_accessed=0, transcendentals=0)


def whole_block(value):
    return pl.BlockSpec(value.shape, lambda *_: (0,) * len(value.shape))


def small_call(
    kernel, name, at, operands, out_shape, scratch=(), waits=(), through=(), cost=1
):
    anywhere = pl.BlockSpec(memory_space=pl.ANY)
    first = 1 + len(operands) + len(waits)
    return pl.pallas_call(
        ordered(kernel, len(operands), len(waits), len(out_shape), len(through)),
        grid=(1,),
        in_specs=[pl.BlockSpec(memory_space=pltpu.SMEM)]
        + [whole_block(value) for value in operands]
        + [anywhere] * len(waits)
        + [pl.BlockSpec(memory_space=pltpu.HBM)] * len(through),
        out_specs=[whole_block(value) for value in out_shape]
        + [pl.BlockSpec(memory_space=pltpu.HBM)] * len(through),
        out_shape=[
            *out_shape,
            *(jax.ShapeDtypeStruct(value.shape, value.dtype) for value in through),
        ],
        input_output_aliases={
            first + index: len(out_shape) + index for index in range(len(through))
        },
        scratch_shapes=list(scratch),
        compiler_params=pltpu.CompilerParams(vmem_limit_bytes=VMEM_GRANT),
        cost_estimate=time_estimate(cost),
        name=name,
    )(at, *operands, *waits, *through)


def mixed_kernel(_, held_ref, passed_ref, out):
    out[0] = held_ref[...]
    out[1] = passed_ref[1]


def go_round(at, pieces):
    own, held, given = pieces
    beside = exchanged(given, 1)
    shape = jax.ShapeDtypeStruct(given.shape, given.dtype)
    (both,) = small_call(mixed_kernel, "mix", at, (held, beside), [shape])
    across = exchanged(both, 2)
    return own, beside, across


def deal_kernel(at_ref, query_ref, cotangent_ref, *refs):
    columns, outs, taken_ref = refs[: -LANES - 1], refs[-LANES - 1 : -1], refs[-1]
    width = outs[0].shape[2]
    for bits, out in enumerate(outs):
        held = at_offset(at_ref[0] ^ bits, width)
        out[0] = query_ref[0, :, held]
        out[1] = cotangent_ref[0, :, held]
    for index, column in enumerate(columns):
        taken_ref[:, index * HEAD_DIM : (index + 1) * HEAD_DIM] = column[...]


def deal(at, queries, upstream, weight):
    _, size, width = queries.shape
    depth = weight.shape[0]
    heads = width // LANES // HEAD_DIM
    piece = jax.ShapeDtypeStruct((2, size, width // LANES), jnp.bfloat16)
    taken = jax.ShapeDtypeStruct((depth, 2 * heads * HEAD_DIM), weight.dtype)

    def column(index):
        first = index % 2 * (width // HEAD_DIM) + index // 2
        return pl.BlockSpec((depth, HEAD_DIM), lambda _, at_ref: (0, first + at_ref[0] * heads))

    outs = pl.pallas_call(
        deal_kernel,
        grid_spec=pltpu.PrefetchScalarGridSpec(
            num_scalar_prefetch=1,
            grid=(1,),
            in_specs=[whole_block(queries), whole_block(upstream)]
            + [column(index) for index in range(2 * heads)],
            out_specs=[whole_block(piece)] * LANES + [whole_block(taken)],
        ),
        out_shape=[piece] * LANES + [taken],
        compiler_params=pltpu.CompilerParams(vmem_limit_bytes=VMEM_GRANT),
        cost_estimate=work_estimate(2),
        name="deal",
    )(at, queries, upstream, *[weight] * (2 * heads))
    return outs[:LANES], outs[LANES]


def take_rows_kernel(_, weight_ref, out_ref):
    out_ref[...] = weight_ref[...]


def take_rows(at, weight):
    shape = (weight.shape[0] // 2, weight.shape[1])
    return pl.pallas_call(
        take_rows_kernel,
        grid_spec=pltpu.PrefetchScalarGridSpec(
            num_scalar_prefetch=1,
            grid=(1,),
            in_specs=[pl.BlockSpec(shape, lambda _, at_ref: (at_ref[2], 0))],
            out_specs=pl.BlockSpec(shape, lambda *_: (0, 0)),
        ),
        out_shape=jax.ShapeDtypeStruct(shape, weight.dtype),
        compiler_params=pltpu.CompilerParams(vmem_limit_bytes=VMEM_GRANT),
        cost_estimate=work_estimate(2),
        name="take_rows",
    )(at, weight)


def place_rows_kernel(at_ref, *refs):
    pieces, outs = refs[:LANES], refs[LANES:]
    size = pieces[0].shape[1]
    for bits, piece in enumerate(pieces):
        for head, out in enumerate(outs):
            column = slice(head * HEAD_DIM, (head + 1) * HEAD_DIM)
            out[:, at_offset(at_ref[0] ^ bits, size)] = piece[:, :, column]


def place_rows(at, pieces, waits, through):
    kinds, size, width = pieces[0].shape
    heads = width // HEAD_DIM
    whole = jax.ShapeDtypeStruct((kinds, LANES * size, HEAD_DIM), pieces[0].dtype)
    outs = small_call(
        place_rows_kernel, "place_rows", at, pieces, [whole] * heads, waits=waits, through=through
    )
    return outs[:heads], outs[heads:]


TOKEN = jax.ShapeDtypeStruct((8, 128), jnp.float32)


def settle_kernel(at_ref, *refs, heads):
    own_outs, arrived, (own, held, given) = refs[:heads], refs[heads], refs[heads + 1 :]
    size = own.shape[1]
    for bits, out in enumerate((own, given.at[0], held, given.at[1])):
        rows = at_offset(at_ref[0] ^ bits, size)
        for head, own_out in enumerate(own_outs):
            column = slice(head * HEAD_DIM, (head + 1) * HEAD_DIM)
            whole = own_out[:, rows] + arrived[:, rows, column].astype(jnp.float32)
            out[:, :, column] = whole.astype(jnp.bfloat16)


def settle_outs(at, own_outs, arrived, waits):
    kinds, count, width = arrived.shape
    piece = jax.ShapeDtypeStruct((kinds, count // LANES, width), jnp.bfloat16)
    pair = jax.ShapeDtypeStruct((2, *piece.shape), jnp.bfloat16)
    return small_call(
        functools.partial(settle_kernel, heads=len(own_outs)),
        "settle_outs", at, (*own_outs, arrived), [piece, piece, pair], waits=waits,
    )


def place_heads_kernel(at_ref, own, beside, across, *outs):
    *outs, token = outs
    token[...] = jnp.zeros_like(token)
    width = own.shape[2]
    for bits, piece in enumerate((own, beside.at[0], across.at[0], across.at[1])):
        column = at_offset(at_ref[0] ^ bits, width)
        for kind, out in enumerate(outs):
            out[0, :, column] = piece[kind]


def place_heads(at, found):
    kinds, size, width = found[0].shape
    whole = jax.ShapeDtypeStruct((1, size, LANES * width), jnp.bfloat16)
    return small_call(place_heads_kernel, "place_heads", at, found, [whole] * kinds + [TOKEN])


def spread_kernel(at_ref, *refs, rows, before):
    tokens, own_ref, arrived_ref = refs[:LANES], refs[LANES], refs[LANES + 1]
    earlier = refs[LANES + 2 : LANES + 2 + before]
    own, held, given, kept_ref, sent_ref = refs[LANES + 2 + before : -2]
    kv_pieces = (own, given.at[0], held, given.at[1])
    if before:
        earlier = (earlier[0], earlier[2].at[0], earlier[1], earlier[2].at[1])
    turned, partial = refs[-2:]
    lane, half = at_ref[0], at_ref[1]
    size, depth = tokens[0].shape
    cols = own_ref.shape[1]
    for bits, piece in enumerate(kv_pieces):
        held = at_offset(lane ^ bits, size)
        kv_grad = (own_ref[held] + arrived_ref[held].astype(jnp.float32)).astype(jnp.bfloat16)
        if before:
            piece[:, : own.shape[1] - cols] = earlier[bits][...]
        piece[:, own.shape[1] - cols :] = kv_grad
        turned[:, bits * size : (bits + 1) * size] = kv_grad.T
    step = 256
    for start in range(0, depth, step):
        found = None
        for bits, piece in enumerate(tokens):
            term = product(turned[:, bits * size : (bits + 1) * size], piece[:, start : start + step])
            found = term if found is None else found + term
        partial[start : start + step] = found.T
    chunk = kept_ref.shape[1]
    for out, side in ((kept_ref, half), (sent_ref, 1 - half)):
        for index in range(rows):
            out[index] = partial[at_offset(side * rows + index, chunk)].astype(out.dtype)


def spread(at, tokens, own_grad, arrived, earlier, rows, waits, through):
    size, depth = tokens[0].shape
    cols = own_grad.shape[1]
    chunk = depth // 2 // rows
    shape = (rows, chunk, cols)
    width = cols + (earlier[0].shape[1] if earlier else 0)
    piece = jax.ShapeDtypeStruct((size, width), jnp.bfloat16)
    outs = small_call(
        functools.partial(spread_kernel, rows=rows, before=len(earlier)),
        "spread", at, (*tokens, own_grad, arrived, *earlier),
        [
            piece,
            piece,
            jax.ShapeDtypeStruct((2, size, width), jnp.bfloat16),
            jax.ShapeDtypeStruct(shape, jnp.float32),
            jax.ShapeDtypeStruct(shape, jnp.bfloat16),
        ],
        [pltpu.VMEM((cols, LANES * size), jnp.bfloat16), pltpu.VMEM((depth, cols), jnp.float32)],
        waits=waits,
        through=through,
        cost=0,
    )
    return outs[:3], outs[3], outs[4], outs[5:]


def feature_kernel(at_ref, *refs, heads, counts):
    (own, beside, across), weights, (out_ref, token, tokens) = refs[:3], refs[3:-3], refs[-3:]
    pieces = (own, beside.at[0], across.at[0], across.at[1])
    step = pl.program_id(0)
    width = tokens.shape[1] // 2

    @pl.when(step == 0)
    def _():
        token[...] = jnp.zeros_like(token)
        for head in range(heads):
            for bits in range(LANES):
                piece = pieces[bits][:, 2 * head * HEAD_DIM : 2 * (head + 1) * HEAD_DIM]
                column = (at_ref[0] ^ bits) * heads + head
                tokens[:, at_offset(column, HEAD_DIM)] = piece[:, :HEAD_DIM]
                tokens[:, at_offset(column + width // HEAD_DIM, HEAD_DIM)] = piece[:, HEAD_DIM:]

    first = 0
    for weight, count in zip(weights, counts):

        @pl.when((step >= first) & (step < first + count))
        def _(weight=weight):
            out_ref[0] = product_minor(tokens[...], weight[...]).astype(jnp.bfloat16)

        first += count


def feature_grads(at, found, weights, waits):
    pieces = found
    size = pieces[0].shape[0]
    heads = pieces[0].shape[1] // (2 * HEAD_DIM)
    step = 512
    counts = [weight.shape[0] // step for weight in weights]
    depth = sum(counts) * step
    starts = [sum(counts[:index]) for index in range(len(counts))]
    side, part = counts[0], counts[1]

    def place(index, at_ref):
        half, core = at_ref[1], at_ref[2]
        other = (1 - half) * side
        fetched = other + core * part + index - starts[1]
        passed = other + (1 - core) * part + index - starts[2]
        return jnp.where(
            index < starts[1],
            half * side + index,
            jnp.where(index < starts[2], fetched, passed),
        )

    def weight_spec(weight, start, count):
        return pl.BlockSpec(
            (step, weight.shape[1]), lambda index, _: (jnp.clip(index - start, 0, count - 1), 0)
        )

    return pl.pallas_call(
        ordered(
            functools.partial(feature_kernel, heads=heads, counts=counts),
            len(pieces) + len(weights),
            len(waits),
            2,
            0,
        ),
        grid_spec=pltpu.PrefetchScalarGridSpec(
            num_scalar_prefetch=1,
            grid=(sum(counts),),
            in_specs=[whole_block(piece) for piece in pieces]
            + [weight_spec(*found) for found in zip(weights, starts, counts)]
            + [pl.BlockSpec(memory_space=pl.ANY)] * len(waits),
            out_specs=[
                pl.BlockSpec((1, size, step), lambda index, at_ref: (0, 0, place(index, at_ref))),
                whole_block(TOKEN),
            ],
            scratch_shapes=[pltpu.VMEM((size, weights[0].shape[1]), jnp.bfloat16)],
        ),
        out_shape=[jax.ShapeDtypeStruct((1, size, depth), jnp.bfloat16), TOKEN],
        compiler_params=pltpu.CompilerParams(vmem_limit_bytes=VMEM_GRANT),
        cost_estimate=time_estimate(6),
        name="feature_grads",
    )(at, *pieces, *weights, *waits)


def place_weight_kernel(at_ref, *refs, heads):
    *pieces, out = refs
    width = out.shape[1] // 2
    for bits, piece in enumerate(pieces):
        for head in range(heads):
            column = (at_ref[0] ^ bits) * heads + head
            start = 2 * head * HEAD_DIM
            out[:, at_offset(column, HEAD_DIM)] = piece[:, start : start + HEAD_DIM]
            out[:, at_offset(column + width // HEAD_DIM, HEAD_DIM)] = piece[
                :, start + HEAD_DIM : start + 2 * HEAD_DIM
            ]


def place_weight(at, pieces, waits):
    count, cols = pieces[0].shape
    whole = jax.ShapeDtypeStruct((count, LANES * cols), jnp.float32)
    return small_call(
        functools.partial(place_weight_kernel, heads=cols // (2 * HEAD_DIM)),
        "place_weight", at, pieces, [whole], waits=waits,
    )[0]


def merge_kernel(at_ref, *refs, place):
    *inputs, kept_ref, sent_ref = refs
    bit = at_ref[place]
    for index in range(kept_ref.shape[0]):
        for out, high in ((kept_ref, bit), (sent_ref, 1 - bit)):
            found = inputs[0][2 * index + high]
            for arrived in inputs[1:]:
                found = found + arrived[2 * index + high].astype(jnp.float32)
            out[index] = found.astype(out.dtype)


def merge(at, place, kept, arrived, waits=()):
    shape = (kept.shape[0] // 2, *kept.shape[1:])
    return small_call(
        functools.partial(merge_kernel, place=place),
        "merge", at, (kept, *arrived),
        [jax.ShapeDtypeStruct(shape, jnp.float32), jax.ShapeDtypeStruct(shape, jnp.bfloat16)],
        waits=waits,
    )


def finish_kernel(at_ref, *refs, heads, each):
    inputs, outs = refs[: heads * each], refs[heads * each : -1]
    total = refs[-1]
    size = outs[0].shape[0]
    cols = inputs[0].shape[2]
    for head in range(heads):
        found = inputs[head * each][0]
        for arrived in inputs[head * each + 1 : (head + 1) * each]:
            found = found + arrived[0].astype(jnp.float32)
        total[:, head * cols : (head + 1) * cols] = found
    for bits, out in enumerate(outs):
        out[...] = total[at_offset(at_ref[0] ^ bits, size)]


def finish(at, parts, waits):
    _, chunk, cols = parts[0][0].shape
    heads = len(parts)
    piece = jax.ShapeDtypeStruct((chunk // LANES, heads * cols), jnp.float32)
    return small_call(
        functools.partial(finish_kernel, heads=heads, each=len(parts[0])),
        "finish", at, [value for part in parts for value in part], [piece] * LANES,
        [pltpu.VMEM((chunk, heads * cols), jnp.float32)],
        waits=waits,
    )


def passed_round(pieces):
    return [exchanged(piece, bits) if bits else piece for bits, piece in enumerate(pieces)]


def local(features, queries, kv_weight, upstream):
    tokens = features[0]
    size = tokens.shape[0]
    weight_rows, kv_width = kv_weight.shape
    width = kv_width // 2
    lane_width = width // LANES
    heads = lane_width // HEAD_DIM
    rows = lax.axis_size("seq") // LANES
    place = lax.axis_index("seq")
    lane = place % LANES
    row = place // LANES
    half = lax.axis_index("dp")
    core = place % 2

    here = jnp.stack([lane, half, core]).astype(jnp.int32)
    pair_pieces, lane_weight = deal(here, queries, upstream, kv_weight)
    other_lane_weight = swapped(lane_weight)
    across = exchanged(tokens, 2)
    beside = exchanged(tokens, 1)
    diagonal = exchanged(across, 1)
    row_tokens = (tokens, beside, across, diagonal)

    owns = project(here, row_tokens, (lane_weight, other_lane_weight))
    windows = [(own, shifted(own, 1)) for own in owns]

    part = take_rows(here, kv_weight)
    own_pairs, (part,) = place_rows(here, passed_round(pair_pieces), owns[:1], (part,))
    next_pairs = [shifted(own_pair, -1) for own_pair in own_pairs]

    fetched = swapped(part)

    at = jnp.stack([row, lane]).astype(jnp.int32)
    shared, turns = [], []
    for head in range(heads):
        turns.append(turned_over(at, windows[head][1]))
        own_stats, next_stats = softmax_stats(
            at, own_pairs[head], next_pairs[head], windows[head], size, (turns[-1],)
        )
        shared.append(
            (own_stats, turned_round(next_stats, 1), next_stats, turned_round(own_stats, -1))
        )
    gained, next_out = [], ()
    for head in range(heads):
        gained.append(
            attention_grads(
                at, own_pairs[head], next_pairs[head], (*windows[head], turns[head]),
                shared[head], next_out, size,
                (shared[-1][0],),
            )
        )
        next_out = (gained[-1][1],)
    own_outs = [found[0] for found in gained]

    bits = jnp.stack([(row >> index) % 2 for index in range(rows.bit_length() - 1)])
    kv_pieces, parts = [], []
    waits, through = (gained[-1][3],), (fetched,)
    arrived_out = shifted(next_out[0], 1)
    for head, (_, _, near_grad, own_grad) in enumerate(gained):
        kv_pieces, kept, sent, handed = spread(
            here, row_tokens, own_grad, shifted(near_grad, -1), kv_pieces, rows, waits, through
        )
        if through:
            (fetched,) = handed
            passed = exchanged(fetched, 1)
        if head == heads - 1:
            kv_found = go_round(here, kv_pieces)
            out_found = go_round(here, settle_outs(here, own_outs, arrived_out, (sent,)))
        waits, through = (), ()
        arrived = [swapped(sent)]
        distance = 1
        while distance < rows:
            last = head == heads - 1 and 2 * distance == rows
            kept, sent = merge(
                bits, distance.bit_length() - 1, kept, arrived, kv_found[2:] if last else ()
            )
            arrived = [moved(sent, distance * LANES, 0)]
            if not waits:
                waits = (sent,)
            distance *= 2
        parts.append((kept, *arrived))

    feature_grad, feature_token = feature_grads(
        here,
        kv_found,
        (kv_weight, fetched, passed),
        (sent,),
    )
    attended, query_grad, token = place_heads(here, out_found)
    pieces = passed_round(finish(here, parts, (feature_token,)))
    weight_grad = place_weight(here, pieces, (token,))
    return (attended, query_grad, feature_grad, weight_grad)


def solution(mesh):
    return jax.shard_map(
        local,
        mesh=mesh,
        in_specs=(P("dp", "seq", None), P("dp", "seq", None), P("dp", None), P("dp", "seq", None)),
        out_specs=(
            P("dp", "seq", None),
            P("dp", "seq", None),
            P("dp", "seq", None),
            P(("dp", "seq"), None),
        ),
        check_vma=False,
    )
```

```python
import functools
import math

import jax
import jax.numpy as jnp
from jax import lax
from jax.experimental import pallas as pl
from jax.experimental.pallas import tpu as pltpu
from jax.sharding import PartitionSpec as P

HEAD_DIM = 128
WINDOW = 2048
LANES = 4
VMEM_GRANT = 24 * 2**20
SCORE_SCALE = 1.0 / math.sqrt(HEAD_DIM)
EXP2_SCALE = SCORE_SCALE * math.log2(math.e)
MASKED = -1e30
MINOR_DIMS = (((1,), (1,)), ((), ()))
MAJOR_DIMS = (((0,), (0,)), ((), ()))


def exchanged(value, bits):
    count = lax.axis_size("seq")
    return lax.ppermute(value, "seq", [(source, source ^ bits) for source in range(count)])


def shifted(value, rows):
    count = lax.axis_size("seq")
    steps = rows * LANES
    leading, last = (max(0, -steps), min(count, count - steps))
    return lax.ppermute(value, "seq", [(source, source + steps) for source in range(leading, last)])


def turned_round(value, rows):
    count = lax.axis_size("seq")
    pairs = [(source, (source + rows * LANES) % count) for source in range(count)]
    return lax.ppermute(value, "seq", pairs)


def moved(value, bits, across):
    count = lax.axis_size("seq")
    pairs = [
        (2 * place + side, 2 * (place ^ bits) + (side ^ across))
        for place in range(count)
        for side in range(2)
    ]
    return lax.ppermute(value, ("seq", "dp"), pairs)


def swapped(value):
    return lax.ppermute(value, "dp", [(0, 1), (1, 0)])


def by_sublane(block, reduce):
    return reduce(block.reshape(block.shape[0] // 8, 8, block.shape[1]), axis=0)


def product(left, right):
    return jnp.dot(left, right, preferred_element_type=jnp.float32)


def product_minor(left, right):
    return lax.dot_general(left, right, MINOR_DIMS, preferred_element_type=jnp.float32)


def project_kernel(at_ref, *refs, heads):
    tokens, here_ref, there_ref, outs = refs[:LANES], refs[LANES], refs[LANES + 1], refs[-heads:]
    lane, half = at_ref[0], at_ref[1]
    depth = here_ref.shape[0]
    for bits, piece in enumerate(tokens):
        here = piece[:, at_offset(half, depth)]
        there = piece[:, at_offset(1 - half, depth)]
        whole = product(here, here_ref[...]) + product(there, there_ref[...])
        held = at_offset(lane ^ bits, piece.shape[0])
        width = whole.shape[1] // heads
        for head, out in enumerate(outs):
            out[held] = whole[:, head * width : (head + 1) * width].astype(jnp.bfloat16)


def project(at, tokens, weights):
    heads = weights[0].shape[1] // (2 * HEAD_DIM)
    whole = jax.ShapeDtypeStruct((LANES * tokens[0].shape[0], 2 * HEAD_DIM), jnp.bfloat16)
    return small_call(
        functools.partial(project_kernel, heads=heads),
        "project", at, (*tokens, *weights), [whole] * heads, cost=4,
    )


def visits(blocks):
    for turn in range(blocks):
        whole = [(1, lane, None) for lane in range(blocks)]
        yield 0, turn, whole + [(0, lane, "low" if lane == turn else None) for lane in range(turn + 1)]
        yield 1, turn, [(1, lane, "high" if lane == turn else None) for lane in range(turn, blocks)]


def masked(score, edge):
    if edge:
        key_pos = lax.broadcasted_iota(jnp.int32, score.shape, 0)
        query_pos = lax.broadcasted_iota(jnp.int32, score.shape, 1)
        allowed = key_pos <= query_pos if edge == "low" else key_pos > query_pos
        score = jnp.where(allowed, score, MASKED)
    return score


def turn_kernel(_, near_ref, out_ref):
    size = out_ref.shape[0]
    for start in range(0, near_ref.shape[0], size):
        out_ref[:, start : start + size] = near_ref[start : start + size].T


def turned_over(at, near):
    shape = jax.ShapeDtypeStruct((near.shape[1], near.shape[0]), near.dtype)
    return small_call(turn_kernel, "turn", at, (near,), [shape])[0]


def stats_kernel(
    at_ref, own_pair, next_pair, own_ref, near_ref, own_out, next_out, scores, *, blocks, size
):
    near_bias = jnp.where(at_ref[0] > 0, 0.0, MASKED)
    window = (own_ref, near_ref)
    pairs = (own_pair, next_pair)
    outs = (own_out, next_out)
    for turn, (side, block, keys) in enumerate(visits(blocks)):
        held = slice(block * size, (block + 1) * size)
        peaks = [jnp.full((8, size), MASKED, jnp.float32)] * 2
        for index, (near, lane, edge) in enumerate(keys):
            key = window[near][lane * size : (lane + 1) * size, :HEAD_DIM]
            score = masked(product_minor(key, pairs[side][0, held]), edge)
            scores[turn % 2, index] = score
            peaks[near] = jnp.maximum(peaks[near], by_sublane(score, jnp.max))
        peaks = [jnp.max(found, axis=0, keepdims=True) for found in peaks]
        peak = jnp.maximum(peaks[0], peaks[1] + near_bias)
        bases = (peak, peak - near_bias)
        mass = jnp.zeros((8, size), jnp.float32)
        pull = jnp.zeros((8, size), jnp.float32)
        for index, (near, lane, edge) in enumerate(keys):
            value = window[near][lane * size : (lane + 1) * size, HEAD_DIM:]
            grown = jnp.exp2((scores[turn % 2, index] - bases[near]) * EXP2_SCALE)
            mass = mass + by_sublane(grown, jnp.sum)
            pull = pull + by_sublane(grown * product_minor(value, pairs[side][1, held]), jnp.sum)
        out = outs[side]
        out[0:1, held] = peak
        out[1:2, held] = jnp.sum(mass, axis=0, keepdims=True)
        out[2:3, held] = jnp.sum(pull, axis=0, keepdims=True)
        out[3:, held] = jnp.zeros((5, size), jnp.float32)


def settled(here, there, there_valid):
    here_peak = here[0:1]
    there_peak = jnp.where(there_valid, there[0:1], MASKED)
    peak = jnp.maximum(here_peak, there_peak)
    here_factor = jnp.exp2((here_peak - peak) * EXP2_SCALE)
    there_factor = jnp.exp2((there_peak - peak) * EXP2_SCALE)
    mass = here[1:2] * here_factor + there[1:2] * there_factor
    pull = here[2:3] * here_factor + there[2:3] * there_factor
    share = jnp.where(mass > 0, 1.0 / mass, 0.0)
    return peak, share, pull * share


def gradient_kernel(
    at_ref, own_pair, next_pair, own_ref, near_ref, near_turned,
    own_stats, far_stats, next_stats, main_stats, *refs, blocks, size,
):
    *earlier, own_out, next_out, near_grad, own_grad = refs[:-7]
    own_turned, queries, cotangents, own_weights, own_dscores, near_weights, near_dscores = refs[-7:]
    turned = (own_turned, near_turned)
    joined = next_out.shape[2] - HEAD_DIM
    if earlier:
        next_out[:, :, :joined] = earlier[0][...]
    near_valid = at_ref[0] > 0
    near_bias = jnp.where(near_valid, 0.0, MASKED)
    window = (own_ref, near_ref)
    row_tokens = blocks * size
    pairs = (own_pair, next_pair)
    outs = (own_out, next_out.at[:, :, joined:])
    weights = (own_weights, near_weights)
    dscores = (own_dscores, near_dscores)
    figures = (
        settled(own_stats[...], far_stats[...], near_valid),
        settled(next_stats[...], main_stats[...], True),
    )
    for side in range(2):
        queries[side * row_tokens : (side + 1) * row_tokens] = pairs[side][0]
        cotangents[side * row_tokens : (side + 1) * row_tokens] = pairs[side][1]
    for block in range(blocks):
        held = slice(block * size, (block + 1) * size)
        own_turned[:, held] = own_ref[held].T
    for side, block, keys in visits(blocks):
        held = slice(block * size, (block + 1) * size)
        column = slice(side * row_tokens + block * size, side * row_tokens + (block + 1) * size)
        peak, share, centre = (figure[:, held] for figure in figures[side])
        scaled = share * SCORE_SCALE
        bases = (peak, peak - near_bias)
        for near, lane, edge in keys:
            rows = slice(lane * size, (lane + 1) * size)
            score = product_minor(window[near][rows, :HEAD_DIM], pairs[side][0, held])
            dprob = product_minor(window[near][rows, HEAD_DIM:], pairs[side][1, held])
            grown = jnp.exp2((masked(score, edge) - bases[near]) * EXP2_SCALE)
            weights[near][rows, column] = (grown * share).astype(jnp.bfloat16)
            dscores[near][rows, column] = (grown * ((dprob - centre) * scaled)).astype(jnp.bfloat16)
        rows = slice(block * size if side else 0, row_tokens)
        attended = product(turned[1][HEAD_DIM:, rows], near_weights[rows, column])
        query_grad = product(turned[1][:HEAD_DIM, rows], near_dscores[rows, column])
        if not side:
            rows = slice(0, (block + 1) * size)
            attended += product(turned[0][HEAD_DIM:, rows], own_weights[rows, column])
            query_grad += product(turned[0][:HEAD_DIM, rows], own_dscores[rows, column])
        outs[side][0, held] = attended.T.astype(outs[side].dtype)
        outs[side][1, held] = query_grad.T.astype(outs[side].dtype)
    for lane in range(blocks):
        rows = slice(lane * size, (lane + 1) * size)
        met = slice(0, row_tokens + (lane + 1) * size)
        near_grad[rows, :HEAD_DIM] = product(near_dscores[rows, met], queries[met]).astype(
            jnp.bfloat16
        )
        near_grad[rows, HEAD_DIM:] = product(near_weights[rows, met], cotangents[met]).astype(
            jnp.bfloat16
        )
        met = slice(lane * size, row_tokens)
        own_grad[rows, :HEAD_DIM] = product(own_dscores[rows, met], queries[met])
        own_grad[rows, HEAD_DIM:] = product(own_weights[rows, met], cotangents[met])


def kernel_call(kernel, name, at, own_pair, next_pair, kvs, stats, out_shape, scratch, size, waits, cost, grant):
    row_tokens = own_pair.shape[1]
    blocks = row_tokens // size

    return pl.pallas_call(
        ordered(
            functools.partial(kernel, blocks=blocks, size=size),
            2 + len(kvs) + len(stats),
            len(waits),
            len(out_shape),
            0,
        ),
        grid_spec=pltpu.PrefetchScalarGridSpec(
            num_scalar_prefetch=1,
            grid=(1,),
            in_specs=[whole_block(value) for value in (own_pair, next_pair, *kvs, *stats)]
            + [pl.BlockSpec(memory_space=pl.ANY)] * len(waits),
            out_specs=[whole_block(value) for value in out_shape],
            scratch_shapes=scratch,
        ),
        out_shape=out_shape,
        compiler_params=pltpu.CompilerParams(vmem_limit_bytes=grant),
        cost_estimate=time_estimate(cost),
        name=name,
    )(at, own_pair, next_pair, *kvs, *stats, *waits)


def softmax_stats(at, own_pair, next_pair, kvs, size, waits):
    row_tokens = own_pair.shape[1]
    return kernel_call(
        stats_kernel, "softmax_stats", at, own_pair, next_pair, kvs, (),
        [jax.ShapeDtypeStruct((8, row_tokens), jnp.float32)] * 2,
        [pltpu.VMEM((2, 2 * row_tokens // size, size, size), jnp.float32)],
        size, waits, 4, 20 * 2**20,
    )


def attention_grads(at, own_pair, next_pair, kvs, stats, earlier, size, waits):
    row_tokens = own_pair.shape[1]
    low = jnp.bfloat16
    width = HEAD_DIM + (earlier[0].shape[2] if earlier else 0)
    return kernel_call(
        gradient_kernel, "attention_grads", at, own_pair, next_pair, kvs, (*stats, *earlier),
        [
            jax.ShapeDtypeStruct((2, row_tokens, HEAD_DIM), jnp.float32),
            jax.ShapeDtypeStruct((2, row_tokens, width), low),
            jax.ShapeDtypeStruct((row_tokens, 2 * HEAD_DIM), low),
            jax.ShapeDtypeStruct((row_tokens, 2 * HEAD_DIM), jnp.float32),
        ],
        [
            pltpu.VMEM((2 * HEAD_DIM, row_tokens), low),
            pltpu.VMEM((2 * row_tokens, HEAD_DIM), low),
            pltpu.VMEM((2 * row_tokens, HEAD_DIM), low),
            pltpu.VMEM((row_tokens, row_tokens), low),
            pltpu.VMEM((row_tokens, row_tokens), low),
            pltpu.VMEM((row_tokens, 2 * row_tokens), low),
            pltpu.VMEM((row_tokens, 2 * row_tokens), low),
        ],
        size, waits, 8, 40 * 2**20,
    )


def at_offset(index, size):
    return pl.ds(pl.multiple_of(index * size, size), size)


def ordered(kernel, inputs, waits, outputs, through):
    def body(*refs):
        first = 1 + inputs + waits + through
        kept = first + outputs
        return kernel(*refs[: 1 + inputs], *refs[first:kept], *refs[kept + through :])

    return body


def time_estimate(microseconds):
    return pl.CostEstimate(
        flops=microseconds * 10**9, bytes_accessed=microseconds * 3 * 10**6, transcendentals=0
    )


def work_estimate(microseconds):
    return pl.CostEstimate(flops=microseconds * 10**9, bytes_accessed=0, transcendentals=0)


def whole_block(value):
    return pl.BlockSpec(value.shape, lambda *_: (0,) * len(value.shape))


def small_call(
    kernel, name, at, operands, out_shape, scratch=(), waits=(), through=(), cost=1
):
    anywhere = pl.BlockSpec(memory_space=pl.ANY)
    first = 1 + len(operands) + len(waits)
    return pl.pallas_call(
        ordered(kernel, len(operands), len(waits), len(out_shape), len(through)),
        grid=(1,),
        in_specs=[pl.BlockSpec(memory_space=pltpu.SMEM)]
        + [whole_block(value) for value in operands]
        + [anywhere] * len(waits)
        + [pl.BlockSpec(memory_space=pltpu.HBM)] * len(through),
        out_specs=[whole_block(value) for value in out_shape]
        + [pl.BlockSpec(memory_space=pltpu.HBM)] * len(through),
        out_shape=[
            *out_shape,
            *(jax.ShapeDtypeStruct(value.shape, value.dtype) for value in through),
        ],
        input_output_aliases={
            first + index: len(out_shape) + index for index in range(len(through))
        },
        scratch_shapes=list(scratch),
        compiler_params=pltpu.CompilerParams(vmem_limit_bytes=VMEM_GRANT),
        cost_estimate=time_estimate(cost),
        name=name,
    )(at, *operands, *waits, *through)


def mixed_kernel(_, held_ref, passed_ref, out):
    out[0] = held_ref[...]
    out[1] = passed_ref[1]


def go_round(at, pieces):
    own, held, given = pieces
    beside = exchanged(given, 1)
    shape = jax.ShapeDtypeStruct(given.shape, given.dtype)
    (both,) = small_call(mixed_kernel, "mix", at, (held, beside), [shape])
    across = exchanged(both, 2)
    return own, beside, across


def deal_kernel(at_ref, query_ref, cotangent_ref, *refs):
    columns, outs, taken_ref = refs[: -LANES - 1], refs[-LANES - 1 : -1], refs[-1]
    width = outs[0].shape[2]
    for bits, out in enumerate(outs):
        held = at_offset(at_ref[0] ^ bits, width)
        out[0] = query_ref[0, :, held]
        out[1] = cotangent_ref[0, :, held]
    for index, column in enumerate(columns):
        taken_ref[:, index * HEAD_DIM : (index + 1) * HEAD_DIM] = column[...]


def deal(at, queries, upstream, weight):
    _, size, width = queries.shape
    depth = weight.shape[0]
    heads = width // LANES // HEAD_DIM
    piece = jax.ShapeDtypeStruct((2, size, width // LANES), jnp.bfloat16)
    taken = jax.ShapeDtypeStruct((depth, 2 * heads * HEAD_DIM), weight.dtype)

    def column(index):
        first = index % 2 * (width // HEAD_DIM) + index // 2
        return pl.BlockSpec((depth, HEAD_DIM), lambda _, at_ref: (0, first + at_ref[0] * heads))

    outs = pl.pallas_call(
        deal_kernel,
        grid_spec=pltpu.PrefetchScalarGridSpec(
            num_scalar_prefetch=1,
            grid=(1,),
            in_specs=[whole_block(queries), whole_block(upstream)]
            + [column(index) for index in range(2 * heads)],
            out_specs=[whole_block(piece)] * LANES + [whole_block(taken)],
        ),
        out_shape=[piece] * LANES + [taken],
        compiler_params=pltpu.CompilerParams(vmem_limit_bytes=VMEM_GRANT),
        cost_estimate=work_estimate(2),
        name="deal",
    )(at, queries, upstream, *[weight] * (2 * heads))
    return outs[:LANES], outs[LANES]


def take_rows_kernel(_, weight_ref, out_ref):
    out_ref[...] = weight_ref[...]


def take_rows(at, weight):
    shape = (weight.shape[0] // 2, weight.shape[1])
    return pl.pallas_call(
        take_rows_kernel,
        grid_spec=pltpu.PrefetchScalarGridSpec(
            num_scalar_prefetch=1,
            grid=(1,),
            in_specs=[pl.BlockSpec(shape, lambda _, at_ref: (at_ref[2], 0))],
            out_specs=pl.BlockSpec(shape, lambda *_: (0, 0)),
        ),
        out_shape=jax.ShapeDtypeStruct(shape, weight.dtype),
        compiler_params=pltpu.CompilerParams(vmem_limit_bytes=VMEM_GRANT),
        cost_estimate=work_estimate(2),
        name="take_rows",
    )(at, weight)


def place_rows_kernel(at_ref, *refs):
    pieces, outs = refs[:LANES], refs[LANES:]
    size = pieces[0].shape[1]
    for bits, piece in enumerate(pieces):
        for head, out in enumerate(outs):
            column = slice(head * HEAD_DIM, (head + 1) * HEAD_DIM)
            out[:, at_offset(at_ref[0] ^ bits, size)] = piece[:, :, column]


def place_rows(at, pieces, waits, through):
    kinds, size, width = pieces[0].shape
    heads = width // HEAD_DIM
    whole = jax.ShapeDtypeStruct((kinds, LANES * size, HEAD_DIM), pieces[0].dtype)
    outs = small_call(
        place_rows_kernel, "place_rows", at, pieces, [whole] * heads, waits=waits, through=through
    )
    return outs[:heads], outs[heads:]


TOKEN = jax.ShapeDtypeStruct((8, 128), jnp.float32)


def settle_kernel(at_ref, *refs, heads):
    own_outs, arrived, (own, held, given) = refs[:heads], refs[heads], refs[heads + 1 :]
    size = own.shape[1]
    for bits, out in enumerate((own, given.at[0], held, given.at[1])):
        rows = at_offset(at_ref[0] ^ bits, size)
        for head, own_out in enumerate(own_outs):
            column = slice(head * HEAD_DIM, (head + 1) * HEAD_DIM)
            whole = own_out[:, rows] + arrived[:, rows, column].astype(jnp.float32)
            out[:, :, column] = whole.astype(jnp.bfloat16)


def settle_outs(at, own_outs, arrived, waits):
    kinds, count, width = arrived.shape
    piece = jax.ShapeDtypeStruct((kinds, count // LANES, width), jnp.bfloat16)
    pair = jax.ShapeDtypeStruct((2, *piece.shape), jnp.bfloat16)
    return small_call(
        functools.partial(settle_kernel, heads=len(own_outs)),
        "settle_outs", at, (*own_outs, arrived), [piece, piece, pair], waits=waits,
    )


def place_heads_kernel(at_ref, own, beside, across, *outs):
    *outs, token = outs
    token[...] = jnp.zeros_like(token)
    width = own.shape[2]
    for bits, piece in enumerate((own, beside.at[0], across.at[0], across.at[1])):
        column = at_offset(at_ref[0] ^ bits, width)
        for kind, out in enumerate(outs):
            out[0, :, column] = piece[kind]


def place_heads(at, found):
    kinds, size, width = found[0].shape
    whole = jax.ShapeDtypeStruct((1, size, LANES * width), jnp.bfloat16)
    return small_call(place_heads_kernel, "place_heads", at, found, [whole] * kinds + [TOKEN])


def spread_kernel(at_ref, *refs, rows, before):
    tokens, own_ref, arrived_ref = refs[:LANES], refs[LANES], refs[LANES + 1]
    earlier = refs[LANES + 2 : LANES + 2 + before]
    own, held, given, kept_ref, sent_ref = refs[LANES + 2 + before : -2]
    kv_pieces = (own, given.at[0], held, given.at[1])
    if before:
        earlier = (earlier[0], earlier[2].at[0], earlier[1], earlier[2].at[1])
    turned, partial = refs[-2:]
    lane, half = at_ref[0], at_ref[1]
    size, depth = tokens[0].shape
    cols = own_ref.shape[1]
    for bits, piece in enumerate(kv_pieces):
        held = at_offset(lane ^ bits, size)
        kv_grad = (own_ref[held] + arrived_ref[held].astype(jnp.float32)).astype(jnp.bfloat16)
        if before:
            piece[:, : own.shape[1] - cols] = earlier[bits][...]
        piece[:, own.shape[1] - cols :] = kv_grad
        turned[:, bits * size : (bits + 1) * size] = kv_grad.T
    step = 256
    for start in range(0, depth, step):
        found = None
        for bits, piece in enumerate(tokens):
            term = product(turned[:, bits * size : (bits + 1) * size], piece[:, start : start + step])
            found = term if found is None else found + term
        partial[start : start + step] = found.T
    chunk = kept_ref.shape[1]
    for out, side in ((kept_ref, half), (sent_ref, 1 - half)):
        for index in range(rows):
            out[index] = partial[at_offset(side * rows + index, chunk)].astype(out.dtype)


def spread(at, tokens, own_grad, arrived, earlier, rows, waits, through):
    size, depth = tokens[0].shape
    cols = own_grad.shape[1]
    chunk = depth // 2 // rows
    shape = (rows, chunk, cols)
    width = cols + (earlier[0].shape[1] if earlier else 0)
    piece = jax.ShapeDtypeStruct((size, width), jnp.bfloat16)
    outs = small_call(
        functools.partial(spread_kernel, rows=rows, before=len(earlier)),
        "spread", at, (*tokens, own_grad, arrived, *earlier),
        [
            piece,
            piece,
            jax.ShapeDtypeStruct((2, size, width), jnp.bfloat16),
            jax.ShapeDtypeStruct(shape, jnp.float32),
            jax.ShapeDtypeStruct(shape, jnp.bfloat16),
        ],
        [pltpu.VMEM((cols, LANES * size), jnp.bfloat16), pltpu.VMEM((depth, cols), jnp.float32)],
        waits=waits,
        through=through,
        cost=0,
    )
    return outs[:3], outs[3], outs[4], outs[5:]


def feature_kernel(at_ref, *refs, heads, counts):
    (own, beside, across), weights, (out_ref, token, tokens) = refs[:3], refs[3:-3], refs[-3:]
    pieces = (own, beside.at[0], across.at[0], across.at[1])
    step = pl.program_id(0)
    width = tokens.shape[1] // 2

    @pl.when(step == 0)
    def _():
        token[...] = jnp.zeros_like(token)
        for head in range(heads):
            for bits in range(LANES):
                piece = pieces[bits][:, 2 * head * HEAD_DIM : 2 * (head + 1) * HEAD_DIM]
                column = (at_ref[0] ^ bits) * heads + head
                tokens[:, at_offset(column, HEAD_DIM)] = piece[:, :HEAD_DIM]
                tokens[:, at_offset(column + width // HEAD_DIM, HEAD_DIM)] = piece[:, HEAD_DIM:]

    first = 0
    for weight, count in zip(weights, counts):

        @pl.when((step >= first) & (step < first + count))
        def _(weight=weight):
            out_ref[0] = product_minor(tokens[...], weight[...]).astype(jnp.bfloat16)

        first += count


def feature_grads(at, found, weights, waits):
    pieces = found
    size = pieces[0].shape[0]
    heads = pieces[0].shape[1] // (2 * HEAD_DIM)
    step = 512
    counts = [weight.shape[0] // step for weight in weights]
    depth = sum(counts) * step
    starts = [sum(counts[:index]) for index in range(len(counts))]
    side, part = counts[0], counts[1]

    def place(index, at_ref):
        half, core = at_ref[1], at_ref[2]
        other = (1 - half) * side
        fetched = other + core * part + index - starts[1]
        passed = other + (1 - core) * part + index - starts[2]
        return jnp.where(
            index < starts[1],
            half * side + index,
            jnp.where(index < starts[2], fetched, passed),
        )

    def weight_spec(weight, start, count):
        return pl.BlockSpec(
            (step, weight.shape[1]), lambda index, _: (jnp.clip(index - start, 0, count - 1), 0)
        )

    return pl.pallas_call(
        ordered(
            functools.partial(feature_kernel, heads=heads, counts=counts),
            len(pieces) + len(weights),
            len(waits),
            2,
            0,
        ),
        grid_spec=pltpu.PrefetchScalarGridSpec(
            num_scalar_prefetch=1,
            grid=(sum(counts),),
            in_specs=[whole_block(piece) for piece in pieces]
            + [weight_spec(*found) for found in zip(weights, starts, counts)]
            + [pl.BlockSpec(memory_space=pl.ANY)] * len(waits),
            out_specs=[
                pl.BlockSpec((1, size, step), lambda index, at_ref: (0, 0, place(index, at_ref))),
                whole_block(TOKEN),
            ],
            scratch_shapes=[pltpu.VMEM((size, weights[0].shape[1]), jnp.bfloat16)],
        ),
        out_shape=[jax.ShapeDtypeStruct((1, size, depth), jnp.bfloat16), TOKEN],
        compiler_params=pltpu.CompilerParams(vmem_limit_bytes=VMEM_GRANT),
        cost_estimate=time_estimate(6),
        name="feature_grads",
    )(at, *pieces, *weights, *waits)


def place_weight_kernel(at_ref, *refs, heads):
    *pieces, out = refs
    width = out.shape[1] // 2
    for bits, piece in enumerate(pieces):
        for head in range(heads):
            column = (at_ref[0] ^ bits) * heads + head
            start = 2 * head * HEAD_DIM
            out[:, at_offset(column, HEAD_DIM)] = piece[:, start : start + HEAD_DIM]
            out[:, at_offset(column + width // HEAD_DIM, HEAD_DIM)] = piece[
                :, start + HEAD_DIM : start + 2 * HEAD_DIM
            ]


def place_weight(at, pieces, waits):
    count, cols = pieces[0].shape
    whole = jax.ShapeDtypeStruct((count, LANES * cols), jnp.float32)
    return small_call(
        functools.partial(place_weight_kernel, heads=cols // (2 * HEAD_DIM)),
        "place_weight", at, pieces, [whole], waits=waits,
    )[0]


def merge_kernel(at_ref, *refs, place):
    *inputs, kept_ref, sent_ref = refs
    bit = at_ref[place]
    for index in range(kept_ref.shape[0]):
        for out, high in ((kept_ref, bit), (sent_ref, 1 - bit)):
            found = inputs[0][2 * index + high]
            for arrived in inputs[1:]:
                found = found + arrived[2 * index + high].astype(jnp.float32)
            out[index] = found.astype(out.dtype)


def merge(at, place, kept, arrived, waits=()):
    shape = (kept.shape[0] // 2, *kept.shape[1:])
    return small_call(
        functools.partial(merge_kernel, place=place),
        "merge", at, (kept, *arrived),
        [jax.ShapeDtypeStruct(shape, jnp.float32), jax.ShapeDtypeStruct(shape, jnp.bfloat16)],
        waits=waits,
    )


def finish_kernel(at_ref, *refs, heads, each):
    inputs, outs = refs[: heads * each], refs[heads * each : -1]
    total = refs[-1]
    size = outs[0].shape[0]
    cols = inputs[0].shape[2]
    for head in range(heads):
        found = inputs[head * each][0]
        for arrived in inputs[head * each + 1 : (head + 1) * each]:
            found = found + arrived[0].astype(jnp.float32)
        total[:, head * cols : (head + 1) * cols] = found
    for bits, out in enumerate(outs):
        out[...] = total[at_offset(at_ref[0] ^ bits, size)]


def finish(at, parts, waits):
    _, chunk, cols = parts[0][0].shape
    heads = len(parts)
    piece = jax.ShapeDtypeStruct((chunk // LANES, heads * cols), jnp.float32)
    return small_call(
        functools.partial(finish_kernel, heads=heads, each=len(parts[0])),
        "finish", at, [value for part in parts for value in part], [piece] * LANES,
        [pltpu.VMEM((chunk, heads * cols), jnp.float32)],
        waits=waits,
    )


def passed_round(pieces):
    return [exchanged(piece, bits) if bits else piece for bits, piece in enumerate(pieces)]


def local(features, queries, kv_weight, upstream):
    tokens = features[0]
    size = tokens.shape[0]
    weight_rows, kv_width = kv_weight.shape
    width = kv_width // 2
    lane_width = width // LANES
    heads = lane_width // HEAD_DIM
    rows = lax.axis_size("seq") // LANES
    place = lax.axis_index("seq")
    lane = place % LANES
    row = place // LANES
    half = lax.axis_index("dp")
    core = place % 2

    here = jnp.stack([lane, half, core]).astype(jnp.int32)
    pair_pieces, lane_weight = deal(here, queries, upstream, kv_weight)
    other_lane_weight = swapped(lane_weight)
    across = exchanged(tokens, 2)
    beside = exchanged(tokens, 1)
    diagonal = exchanged(across, 1)
    row_tokens = (tokens, beside, across, diagonal)

    owns = project(here, row_tokens, (lane_weight, other_lane_weight))
    windows = [(own, shifted(own, 1)) for own in owns]

    part = take_rows(here, kv_weight)
    own_pairs, (part,) = place_rows(here, passed_round(pair_pieces), owns[:1], (part,))
    next_pairs = [shifted(own_pair, -1) for own_pair in own_pairs]

    fetched = swapped(part)

    at = jnp.stack([row, lane]).astype(jnp.int32)
    shared, turns = [], []
    for head in range(heads):
        turns.append(turned_over(at, windows[head][1]))
        own_stats, next_stats = softmax_stats(
            at, own_pairs[head], next_pairs[head], windows[head], size, (turns[-1],)
        )
        shared.append(
            (own_stats, turned_round(next_stats, 1), next_stats, turned_round(own_stats, -1))
        )
    gained, next_out = [], ()
    for head in range(heads):
        gained.append(
            attention_grads(
                at, own_pairs[head], next_pairs[head], (*windows[head], turns[head]),
                shared[head], next_out, size,
                (shared[-1][0],),
            )
        )
        next_out = (gained[-1][1],)
    own_outs = [found[0] for found in gained]

    bits = jnp.stack([(row >> index) % 2 for index in range(rows.bit_length() - 1)])
    kv_pieces, parts = [], []
    waits, through = (gained[-1][3],), (fetched,)
    arrived_out = shifted(next_out[0], 1)
    for head, (_, _, near_grad, own_grad) in enumerate(gained):
        kv_pieces, kept, sent, handed = spread(
            here, row_tokens, own_grad, shifted(near_grad, -1), kv_pieces, rows, waits, through
        )
        if through:
            (fetched,) = handed
            passed = exchanged(fetched, 1)
        if head == heads - 1:
            kv_found = go_round(here, kv_pieces)
            out_found = go_round(here, settle_outs(here, own_outs, arrived_out, (sent,)))
        waits, through = (), ()
        arrived = [swapped(sent)]
        distance = 1
        while distance < rows:
            last = head == heads - 1 and 2 * distance == rows
            kept, sent = merge(
                bits, distance.bit_length() - 1, kept, arrived, kv_found[2:] if last else ()
            )
            arrived = [moved(sent, distance * LANES, 0)]
            if not waits:
                waits = (sent,)
            distance *= 2
        parts.append((kept, *arrived))

    feature_grad, feature_token = feature_grads(
        here,
        kv_found,
        (kv_weight, fetched, passed),
        (sent,),
    )
    attended, query_grad, token = place_heads(here, out_found)
    pieces = passed_round(finish(here, parts, (feature_token,)))
    weight_grad = place_weight(here, pieces, (token,))
    return (attended, query_grad, feature_grad, weight_grad)


def solution(mesh):
    return jax.shard_map(
        local,
        mesh=mesh,
        in_specs=(P("dp", "seq", None), P("dp", "seq", None), P("dp", None), P("dp", "seq", None)),
        out_specs=(
            P("dp", "seq", None),
            P("dp", "seq", None),
            P("dp", "seq", None),
            P(("dp", "seq"), None),
        ),
        check_vma=False,
    )
```

```python
import functools
import math

import jax
import jax.numpy as jnp
from jax import lax
from jax.experimental import pallas as pl
from jax.experimental.pallas import tpu as pltpu
from jax.sharding import PartitionSpec as P

HEAD_DIM = 128
WINDOW = 2048
LANES = 4
VMEM_GRANT = 24 * 2**20
SCORE_SCALE = 1.0 / math.sqrt(HEAD_DIM)
EXP2_SCALE = SCORE_SCALE * math.log2(math.e)
MASKED = -1e30
MINOR_DIMS = (((1,), (1,)), ((), ()))
MAJOR_DIMS = (((0,), (0,)), ((), ()))


def exchanged(value, bits):
    count = lax.axis_size("seq")
    return lax.ppermute(value, "seq", [(source, source ^ bits) for source in range(count)])


def shifted(value, rows):
    count = lax.axis_size("seq")
    steps = rows * LANES
    leading, last = (max(0, -steps), min(count, count - steps))
    return lax.ppermute(value, "seq", [(source, source + steps) for source in range(leading, last)])


def turned_round(value, rows):
    count = lax.axis_size("seq")
    pairs = [(source, (source + rows * LANES) % count) for source in range(count)]
    return lax.ppermute(value, "seq", pairs)


def moved(value, bits, across):
    count = lax.axis_size("seq")
    pairs = [
        (2 * place + side, 2 * (place ^ bits) + (side ^ across))
        for place in range(count)
        for side in range(2)
    ]
    return lax.ppermute(value, ("seq", "dp"), pairs)


def swapped(value):
    return lax.ppermute(value, "dp", [(0, 1), (1, 0)])


def by_sublane(block, reduce):
    return reduce(block.reshape(block.shape[0] // 8, 8, block.shape[1]), axis=0)


def product(left, right):
    return jnp.dot(left, right, preferred_element_type=jnp.float32)


def product_minor(left, right):
    return lax.dot_general(left, right, MINOR_DIMS, preferred_element_type=jnp.float32)


def project_kernel(at_ref, *refs, heads):
    tokens, here_ref, there_ref, outs = refs[:LANES], refs[LANES], refs[LANES + 1], refs[-heads:]
    lane, half = at_ref[0], at_ref[1]
    depth = here_ref.shape[0]
    for bits, piece in enumerate(tokens):
        here = piece[:, at_offset(half, depth)]
        there = piece[:, at_offset(1 - half, depth)]
        whole = product(here, here_ref[...]) + product(there, there_ref[...])
        held = at_offset(lane ^ bits, piece.shape[0])
        width = whole.shape[1] // heads
        for head, out in enumerate(outs):
            out[held] = whole[:, head * width : (head + 1) * width].astype(jnp.bfloat16)


def project(at, tokens, weights):
    heads = weights[0].shape[1] // (2 * HEAD_DIM)
    whole = jax.ShapeDtypeStruct((LANES * tokens[0].shape[0], 2 * HEAD_DIM), jnp.bfloat16)
    return small_call(
        functools.partial(project_kernel, heads=heads),
        "project", at, (*tokens, *weights), [whole] * heads, cost=4,
    )


def visits(blocks):
    for turn in range(blocks):
        whole = [(1, lane, None) for lane in range(blocks)]
        yield 0, turn, whole + [(0, lane, "low" if lane == turn else None) for lane in range(turn + 1)]
        yield 1, turn, [(1, lane, "high" if lane == turn else None) for lane in range(turn, blocks)]


def masked(score, edge):
    if edge:
        key_pos = lax.broadcasted_iota(jnp.int32, score.shape, 0)
        query_pos = lax.broadcasted_iota(jnp.int32, score.shape, 1)
        allowed = key_pos <= query_pos if edge == "low" else key_pos > query_pos
        score = jnp.where(allowed, score, MASKED)
    return score


def turn_kernel(_, near_ref, out_ref):
    size = out_ref.shape[0]
    for start in range(0, near_ref.shape[0], size):
        out_ref[:, start : start + size] = near_ref[start : start + size].T


def turned_over(at, near):
    shape = jax.ShapeDtypeStruct((near.shape[1], near.shape[0]), near.dtype)
    return small_call(turn_kernel, "turn", at, (near,), [shape])[0]


def stats_kernel(
    at_ref, own_pair, next_pair, own_ref, near_ref, own_out, next_out, scores, *, blocks, size
):
    near_bias = jnp.where(at_ref[0] > 0, 0.0, MASKED)
    window = (own_ref, near_ref)
    pairs = (own_pair, next_pair)
    outs = (own_out, next_out)
    for turn, (side, block, keys) in enumerate(visits(blocks)):
        held = slice(block * size, (block + 1) * size)
        peaks = [jnp.full((8, size), MASKED, jnp.float32)] * 2
        for index, (near, lane, edge) in enumerate(keys):
            key = window[near][lane * size : (lane + 1) * size, :HEAD_DIM]
            score = masked(product_minor(key, pairs[side][0, held]), edge)
            scores[turn % 2, index] = score
            peaks[near] = jnp.maximum(peaks[near], by_sublane(score, jnp.max))
        peaks = [jnp.max(found, axis=0, keepdims=True) for found in peaks]
        peak = jnp.maximum(peaks[0], peaks[1] + near_bias)
        bases = (peak, peak - near_bias)
        mass = jnp.zeros((8, size), jnp.float32)
        pull = jnp.zeros((8, size), jnp.float32)
        for index, (near, lane, edge) in enumerate(keys):
            value = window[near][lane * size : (lane + 1) * size, HEAD_DIM:]
            grown = jnp.exp2((scores[turn % 2, index] - bases[near]) * EXP2_SCALE)
            mass = mass + by_sublane(grown, jnp.sum)
            pull = pull + by_sublane(grown * product_minor(value, pairs[side][1, held]), jnp.sum)
        out = outs[side]
        out[0:1, held] = peak
        out[1:2, held] = jnp.sum(mass, axis=0, keepdims=True)
        out[2:3, held] = jnp.sum(pull, axis=0, keepdims=True)
        out[3:, held] = jnp.zeros((5, size), jnp.float32)


def settled(here, there, there_valid):
    here_peak = here[0:1]
    there_peak = jnp.where(there_valid, there[0:1], MASKED)
    peak = jnp.maximum(here_peak, there_peak)
    here_factor = jnp.exp2((here_peak - peak) * EXP2_SCALE)
    there_factor = jnp.exp2((there_peak - peak) * EXP2_SCALE)
    mass = here[1:2] * here_factor + there[1:2] * there_factor
    pull = here[2:3] * here_factor + there[2:3] * there_factor
    share = jnp.where(mass > 0, 1.0 / mass, 0.0)
    return peak, share, pull * share


def gradient_kernel(
    at_ref, own_pair, next_pair, own_ref, near_ref, near_turned,
    own_stats, far_stats, next_stats, main_stats, *refs, blocks, size,
):
    *earlier, own_out, next_out, near_grad, own_grad = refs[:-7]
    own_turned, queries, cotangents, own_weights, own_dscores, near_weights, near_dscores = refs[-7:]
    turned = (own_turned, near_turned)
    joined = next_out.shape[2] - HEAD_DIM
    if earlier:
        next_out[:, :, :joined] = earlier[0][...]
    near_valid = at_ref[0] > 0
    near_bias = jnp.where(near_valid, 0.0, MASKED)
    window = (own_ref, near_ref)
    row_tokens = blocks * size
    pairs = (own_pair, next_pair)
    outs = (own_out, next_out.at[:, :, joined:])
    weights = (own_weights, near_weights)
    dscores = (own_dscores, near_dscores)
    figures = (
        settled(own_stats[...], far_stats[...], near_valid),
        settled(next_stats[...], main_stats[...], True),
    )
    for side in range(2):
        queries[side * row_tokens : (side + 1) * row_tokens] = pairs[side][0]
        cotangents[side * row_tokens : (side + 1) * row_tokens] = pairs[side][1]
    for block in range(blocks):
        held = slice(block * size, (block + 1) * size)
        own_turned[:, held] = own_ref[held].T
    for side, block, keys in visits(blocks):
        held = slice(block * size, (block + 1) * size)
        column = slice(side * row_tokens + block * size, side * row_tokens + (block + 1) * size)
        peak, share, centre = (figure[:, held] for figure in figures[side])
        scaled = share * SCORE_SCALE
        bases = (peak, peak - near_bias)
        for near, lane, edge in keys:
            rows = slice(lane * size, (lane + 1) * size)
            score = product_minor(window[near][rows, :HEAD_DIM], pairs[side][0, held])
            dprob = product_minor(window[near][rows, HEAD_DIM:], pairs[side][1, held])
            grown = jnp.exp2((masked(score, edge) - bases[near]) * EXP2_SCALE)
            weights[near][rows, column] = (grown * share).astype(jnp.bfloat16)
            dscores[near][rows, column] = (grown * ((dprob - centre) * scaled)).astype(jnp.bfloat16)
        rows = slice(block * size if side else 0, row_tokens)
        attended = product(turned[1][HEAD_DIM:, rows], near_weights[rows, column])
        query_grad = product(turned[1][:HEAD_DIM, rows], near_dscores[rows, column])
        if not side:
            rows = slice(0, (block + 1) * size)
            attended += product(turned[0][HEAD_DIM:, rows], own_weights[rows, column])
            query_grad += product(turned[0][:HEAD_DIM, rows], own_dscores[rows, column])
        outs[side][0, held] = attended.T.astype(outs[side].dtype)
        outs[side][1, held] = query_grad.T.astype(outs[side].dtype)
    for lane in range(blocks):
        rows = slice(lane * size, (lane + 1) * size)
        met = slice(0, row_tokens + (lane + 1) * size)
        near_grad[rows, :HEAD_DIM] = product(near_dscores[rows, met], queries[met]).astype(
            jnp.bfloat16
        )
        near_grad[rows, HEAD_DIM:] = product(near_weights[rows, met], cotangents[met]).astype(
            jnp.bfloat16
        )
        met = slice(lane * size, row_tokens)
        own_grad[rows, :HEAD_DIM] = product(own_dscores[rows, met], queries[met])
        own_grad[rows, HEAD_DIM:] = product(own_weights[rows, met], cotangents[met])


def kernel_call(kernel, name, at, own_pair, next_pair, kvs, stats, out_shape, scratch, size, waits, cost, grant):
    row_tokens = own_pair.shape[1]
    blocks = row_tokens // size

    return pl.pallas_call(
        ordered(
            functools.partial(kernel, blocks=blocks, size=size),
            2 + len(kvs) + len(stats),
            len(waits),
            len(out_shape),
            0,
        ),
        grid_spec=pltpu.PrefetchScalarGridSpec(
            num_scalar_prefetch=1,
            grid=(1,),
            in_specs=[whole_block(value) for value in (own_pair, next_pair, *kvs, *stats)]
            + [pl.BlockSpec(memory_space=pl.ANY)] * len(waits),
            out_specs=[whole_block(value) for value in out_shape],
            scratch_shapes=scratch,
        ),
        out_shape=out_shape,
        compiler_params=pltpu.CompilerParams(vmem_limit_bytes=grant),
        cost_estimate=time_estimate(cost),
        name=name,
    )(at, own_pair, next_pair, *kvs, *stats, *waits)


def softmax_stats(at, own_pair, next_pair, kvs, size, waits):
    row_tokens = own_pair.shape[1]
    return kernel_call(
        stats_kernel, "softmax_stats", at, own_pair, next_pair, kvs, (),
        [jax.ShapeDtypeStruct((8, row_tokens), jnp.float32)] * 2,
        [pltpu.VMEM((2, 2 * row_tokens // size, size, size), jnp.float32)],
        size, waits, 4, 20 * 2**20,
    )


def attention_grads(at, own_pair, next_pair, kvs, stats, earlier, size, waits):
    row_tokens = own_pair.shape[1]
    low = jnp.bfloat16
    width = HEAD_DIM + (earlier[0].shape[2] if earlier else 0)
    return kernel_call(
        gradient_kernel, "attention_grads", at, own_pair, next_pair, kvs, (*stats, *earlier),
        [
            jax.ShapeDtypeStruct((2, row_tokens, HEAD_DIM), low),
            jax.ShapeDtypeStruct((2, row_tokens, width), low),
            jax.ShapeDtypeStruct((row_tokens, 2 * HEAD_DIM), low),
            jax.ShapeDtypeStruct((row_tokens, 2 * HEAD_DIM), jnp.float32),
        ],
        [
            pltpu.VMEM((2 * HEAD_DIM, row_tokens), low),
            pltpu.VMEM((2 * row_tokens, HEAD_DIM), low),
            pltpu.VMEM((2 * row_tokens, HEAD_DIM), low),
            pltpu.VMEM((row_tokens, row_tokens), low),
            pltpu.VMEM((row_tokens, row_tokens), low),
            pltpu.VMEM((row_tokens, 2 * row_tokens), low),
            pltpu.VMEM((row_tokens, 2 * row_tokens), low),
        ],
        size, waits, 8, 40 * 2**20,
    )


def at_offset(index, size):
    return pl.ds(pl.multiple_of(index * size, size), size)


def ordered(kernel, inputs, waits, outputs, through):
    def body(*refs):
        first = 1 + inputs + waits + through
        kept = first + outputs
        return kernel(*refs[: 1 + inputs], *refs[first:kept], *refs[kept + through :])

    return body


def time_estimate(microseconds):
    return pl.CostEstimate(
        flops=microseconds * 10**9, bytes_accessed=microseconds * 3 * 10**6, transcendentals=0
    )


def work_estimate(microseconds):
    return pl.CostEstimate(flops=microseconds * 10**9, bytes_accessed=0, transcendentals=0)


def whole_block(value):
    return pl.BlockSpec(value.shape, lambda *_: (0,) * len(value.shape))


def small_call(
    kernel, name, at, operands, out_shape, scratch=(), waits=(), through=(), cost=1
):
    anywhere = pl.BlockSpec(memory_space=pl.ANY)
    first = 1 + len(operands) + len(waits)
    return pl.pallas_call(
        ordered(kernel, len(operands), len(waits), len(out_shape), len(through)),
        grid=(1,),
        in_specs=[pl.BlockSpec(memory_space=pltpu.SMEM)]
        + [whole_block(value) for value in operands]
        + [anywhere] * len(waits)
        + [pl.BlockSpec(memory_space=pltpu.HBM)] * len(through),
        out_specs=[whole_block(value) for value in out_shape]
        + [pl.BlockSpec(memory_space=pltpu.HBM)] * len(through),
        out_shape=[
            *out_shape,
            *(jax.ShapeDtypeStruct(value.shape, value.dtype) for value in through),
        ],
        input_output_aliases={
            first + index: len(out_shape) + index for index in range(len(through))
        },
        scratch_shapes=list(scratch),
        compiler_params=pltpu.CompilerParams(vmem_limit_bytes=VMEM_GRANT),
        cost_estimate=time_estimate(cost),
        name=name,
    )(at, *operands, *waits, *through)


def mixed_kernel(_, held_ref, passed_ref, out):
    out[0] = held_ref[...]
    out[1] = passed_ref[1]


def go_round(at, pieces):
    own, held, given = pieces
    beside = exchanged(given, 1)
    shape = jax.ShapeDtypeStruct(given.shape, given.dtype)
    (both,) = small_call(mixed_kernel, "mix", at, (held, beside), [shape])
    across = exchanged(both, 2)
    return own, beside, across


def deal_kernel(at_ref, query_ref, cotangent_ref, *refs):
    columns, outs, taken_ref = refs[: -LANES - 1], refs[-LANES - 1 : -1], refs[-1]
    width = outs[0].shape[2]
    for bits, out in enumerate(outs):
        held = at_offset(at_ref[0] ^ bits, width)
        out[0] = query_ref[0, :, held]
        out[1] = cotangent_ref[0, :, held]
    for index, column in enumerate(columns):
        taken_ref[:, index * HEAD_DIM : (index + 1) * HEAD_DIM] = column[...]


def deal(at, queries, upstream, weight):
    _, size, width = queries.shape
    depth = weight.shape[0]
    heads = width // LANES // HEAD_DIM
    piece = jax.ShapeDtypeStruct((2, size, width // LANES), jnp.bfloat16)
    taken = jax.ShapeDtypeStruct((depth, 2 * heads * HEAD_DIM), weight.dtype)

    def column(index):
        first = index % 2 * (width // HEAD_DIM) + index // 2
        return pl.BlockSpec((depth, HEAD_DIM), lambda _, at_ref: (0, first + at_ref[0] * heads))

    outs = pl.pallas_call(
        deal_kernel,
        grid_spec=pltpu.PrefetchScalarGridSpec(
            num_scalar_prefetch=1,
            grid=(1,),
            in_specs=[whole_block(queries), whole_block(upstream)]
            + [column(index) for index in range(2 * heads)],
            out_specs=[whole_block(piece)] * LANES + [whole_block(taken)],
        ),
        out_shape=[piece] * LANES + [taken],
        compiler_params=pltpu.CompilerParams(vmem_limit_bytes=VMEM_GRANT),
        cost_estimate=work_estimate(2),
        name="deal",
    )(at, queries, upstream, *[weight] * (2 * heads))
    return outs[:LANES], outs[LANES]


def take_rows_kernel(_, weight_ref, out_ref):
    out_ref[...] = weight_ref[...]


def take_rows(at, weight):
    shape = (weight.shape[0] // 2, weight.shape[1])
    return pl.pallas_call(
        take_rows_kernel,
        grid_spec=pltpu.PrefetchScalarGridSpec(
            num_scalar_prefetch=1,
            grid=(1,),
            in_specs=[pl.BlockSpec(shape, lambda _, at_ref: (at_ref[2], 0))],
            out_specs=pl.BlockSpec(shape, lambda *_: (0, 0)),
        ),
        out_shape=jax.ShapeDtypeStruct(shape, weight.dtype),
        compiler_params=pltpu.CompilerParams(vmem_limit_bytes=VMEM_GRANT),
        cost_estimate=work_estimate(2),
        name="take_rows",
    )(at, weight)


def place_rows_kernel(at_ref, *refs):
    pieces, outs = refs[:LANES], refs[LANES:]
    size = pieces[0].shape[1]
    for bits, piece in enumerate(pieces):
        for head, out in enumerate(outs):
            column = slice(head * HEAD_DIM, (head + 1) * HEAD_DIM)
            out[:, at_offset(at_ref[0] ^ bits, size)] = piece[:, :, column]


def place_rows(at, pieces, waits, through):
    kinds, size, width = pieces[0].shape
    heads = width // HEAD_DIM
    whole = jax.ShapeDtypeStruct((kinds, LANES * size, HEAD_DIM), pieces[0].dtype)
    outs = small_call(
        place_rows_kernel, "place_rows", at, pieces, [whole] * heads, waits=waits, through=through
    )
    return outs[:heads], outs[heads:]


TOKEN = jax.ShapeDtypeStruct((8, 128), jnp.float32)


def settle_kernel(at_ref, *refs, heads):
    own_outs, arrived, (own, held, given) = refs[:heads], refs[heads], refs[heads + 1 :]
    size = own.shape[1]
    for bits, out in enumerate((own, given.at[0], held, given.at[1])):
        rows = at_offset(at_ref[0] ^ bits, size)
        for head, own_out in enumerate(own_outs):
            column = slice(head * HEAD_DIM, (head + 1) * HEAD_DIM)
            whole = own_out[:, rows].astype(jnp.float32)
            whole = whole + arrived[:, rows, column].astype(jnp.float32)
            out[:, :, column] = whole.astype(jnp.bfloat16)


def settle_outs(at, own_outs, arrived, waits):
    kinds, count, width = arrived.shape
    piece = jax.ShapeDtypeStruct((kinds, count // LANES, width), jnp.bfloat16)
    pair = jax.ShapeDtypeStruct((2, *piece.shape), jnp.bfloat16)
    return small_call(
        functools.partial(settle_kernel, heads=len(own_outs)),
        "settle_outs", at, (*own_outs, arrived), [piece, piece, pair], waits=waits,
    )


def place_heads_kernel(at_ref, own, beside, across, *outs):
    *outs, token = outs
    token[...] = jnp.zeros_like(token)
    width = own.shape[2]
    for bits, piece in enumerate((own, beside.at[0], across.at[0], across.at[1])):
        column = at_offset(at_ref[0] ^ bits, width)
        for kind, out in enumerate(outs):
            out[0, :, column] = piece[kind]


def place_heads(at, found):
    kinds, size, width = found[0].shape
    whole = jax.ShapeDtypeStruct((1, size, LANES * width), jnp.bfloat16)
    return small_call(place_heads_kernel, "place_heads", at, found, [whole] * kinds + [TOKEN])


def spread_kernel(at_ref, *refs, rows, before):
    tokens, own_ref, arrived_ref = refs[:LANES], refs[LANES], refs[LANES + 1]
    earlier = refs[LANES + 2 : LANES + 2 + before]
    own, held, given, kept_ref, sent_ref = refs[LANES + 2 + before : -2]
    kv_pieces = (own, given.at[0], held, given.at[1])
    if before:
        earlier = (earlier[0], earlier[2].at[0], earlier[1], earlier[2].at[1])
    turned, partial = refs[-2:]
    lane, half = at_ref[0], at_ref[1]
    size, depth = tokens[0].shape
    cols = own_ref.shape[1]
    for bits, piece in enumerate(kv_pieces):
        held = at_offset(lane ^ bits, size)
        kv_grad = (own_ref[held] + arrived_ref[held].astype(jnp.float32)).astype(jnp.bfloat16)
        if before:
            piece[:, : own.shape[1] - cols] = earlier[bits][...]
        piece[:, own.shape[1] - cols :] = kv_grad
        turned[:, bits * size : (bits + 1) * size] = kv_grad.T
    step = 256
    for start in range(0, depth, step):
        found = None
        for bits, piece in enumerate(tokens):
            term = product(turned[:, bits * size : (bits + 1) * size], piece[:, start : start + step])
            found = term if found is None else found + term
        partial[start : start + step] = found.T
    chunk = kept_ref.shape[1]
    for out, side in ((kept_ref, half), (sent_ref, 1 - half)):
        for index in range(rows):
            out[index] = partial[at_offset(side * rows + index, chunk)].astype(out.dtype)


def spread(at, tokens, own_grad, arrived, earlier, rows, waits, through):
    size, depth = tokens[0].shape
    cols = own_grad.shape[1]
    chunk = depth // 2 // rows
    shape = (rows, chunk, cols)
    width = cols + (earlier[0].shape[1] if earlier else 0)
    piece = jax.ShapeDtypeStruct((size, width), jnp.bfloat16)
    outs = small_call(
        functools.partial(spread_kernel, rows=rows, before=len(earlier)),
        "spread", at, (*tokens, own_grad, arrived, *earlier),
        [
            piece,
            piece,
            jax.ShapeDtypeStruct((2, size, width), jnp.bfloat16),
            jax.ShapeDtypeStruct(shape, jnp.float32),
            jax.ShapeDtypeStruct(shape, jnp.bfloat16),
        ],
        [pltpu.VMEM((cols, LANES * size), jnp.bfloat16), pltpu.VMEM((depth, cols), jnp.float32)],
        waits=waits,
        through=through,
        cost=0,
    )
    return outs[:3], outs[3], outs[4], outs[5:]


def feature_kernel(at_ref, *refs, heads, counts):
    (own, beside, across), weights, (out_ref, token, tokens) = refs[:3], refs[3:-3], refs[-3:]
    pieces = (own, beside.at[0], across.at[0], across.at[1])
    step = pl.program_id(0)
    width = tokens.shape[1] // 2

    @pl.when(step == 0)
    def _():
        token[...] = jnp.zeros_like(token)
        for head in range(heads):
            for bits in range(LANES):
                piece = pieces[bits][:, 2 * head * HEAD_DIM : 2 * (head + 1) * HEAD_DIM]
                column = (at_ref[0] ^ bits) * heads + head
                tokens[:, at_offset(column, HEAD_DIM)] = piece[:, :HEAD_DIM]
                tokens[:, at_offset(column + width // HEAD_DIM, HEAD_DIM)] = piece[:, HEAD_DIM:]

    first = 0
    for weight, count in zip(weights, counts):

        @pl.when((step >= first) & (step < first + count))
        def _(weight=weight):
            out_ref[0] = product_minor(tokens[...], weight[...]).astype(jnp.bfloat16)

        first += count


def feature_grads(at, found, weights, waits):
    pieces = found
    size = pieces[0].shape[0]
    heads = pieces[0].shape[1] // (2 * HEAD_DIM)
    step = 512
    counts = [weight.shape[0] // step for weight in weights]
    depth = sum(counts) * step
    starts = [sum(counts[:index]) for index in range(len(counts))]
    side, part = counts[0], counts[1]

    def place(index, at_ref):
        half, core = at_ref[1], at_ref[2]
        other = (1 - half) * side
        fetched = other + core * part + index - starts[1]
        passed = other + (1 - core) * part + index - starts[2]
        return jnp.where(
            index < starts[1],
            half * side + index,
            jnp.where(index < starts[2], fetched, passed),
        )

    def weight_spec(weight, start, count):
        return pl.BlockSpec(
            (step, weight.shape[1]), lambda index, _: (jnp.clip(index - start, 0, count - 1), 0)
        )

    return pl.pallas_call(
        ordered(
            functools.partial(feature_kernel, heads=heads, counts=counts),
            len(pieces) + len(weights),
            len(waits),
            2,
            0,
        ),
        grid_spec=pltpu.PrefetchScalarGridSpec(
            num_scalar_prefetch=1,
            grid=(sum(counts),),
            in_specs=[whole_block(piece) for piece in pieces]
            + [weight_spec(*found) for found in zip(weights, starts, counts)]
            + [pl.BlockSpec(memory_space=pl.ANY)] * len(waits),
            out_specs=[
                pl.BlockSpec((1, size, step), lambda index, at_ref: (0, 0, place(index, at_ref))),
                whole_block(TOKEN),
            ],
            scratch_shapes=[pltpu.VMEM((size, weights[0].shape[1]), jnp.bfloat16)],
        ),
        out_shape=[jax.ShapeDtypeStruct((1, size, depth), jnp.bfloat16), TOKEN],
        compiler_params=pltpu.CompilerParams(vmem_limit_bytes=VMEM_GRANT),
        cost_estimate=time_estimate(6),
        name="feature_grads",
    )(at, *pieces, *weights, *waits)


def place_weight_kernel(at_ref, *refs, heads):
    *pieces, out = refs
    width = out.shape[1] // 2
    for bits, piece in enumerate(pieces):
        for head in range(heads):
            column = (at_ref[0] ^ bits) * heads + head
            start = 2 * head * HEAD_DIM
            out[:, at_offset(column, HEAD_DIM)] = piece[:, start : start + HEAD_DIM]
            out[:, at_offset(column + width // HEAD_DIM, HEAD_DIM)] = piece[
                :, start + HEAD_DIM : start + 2 * HEAD_DIM
            ]


def place_weight(at, pieces, waits):
    count, cols = pieces[0].shape
    whole = jax.ShapeDtypeStruct((count, LANES * cols), jnp.float32)
    return small_call(
        functools.partial(place_weight_kernel, heads=cols // (2 * HEAD_DIM)),
        "place_weight", at, pieces, [whole], waits=waits,
    )[0]


def merge_kernel(at_ref, *refs, place):
    *inputs, kept_ref, sent_ref = refs
    bit = at_ref[place]
    for index in range(kept_ref.shape[0]):
        for out, high in ((kept_ref, bit), (sent_ref, 1 - bit)):
            found = inputs[0][2 * index + high]
            for arrived in inputs[1:]:
                found = found + arrived[2 * index + high].astype(jnp.float32)
            out[index] = found.astype(out.dtype)


def merge(at, place, kept, arrived, waits=()):
    shape = (kept.shape[0] // 2, *kept.shape[1:])
    return small_call(
        functools.partial(merge_kernel, place=place),
        "merge", at, (kept, *arrived),
        [jax.ShapeDtypeStruct(shape, jnp.float32), jax.ShapeDtypeStruct(shape, jnp.bfloat16)],
        waits=waits,
    )


def finish_kernel(at_ref, *refs, heads, each):
    inputs, outs = refs[: heads * each], refs[heads * each : -1]
    total = refs[-1]
    size = outs[0].shape[0]
    cols = inputs[0].shape[2]
    for head in range(heads):
        found = inputs[head * each][0]
        for arrived in inputs[head * each + 1 : (head + 1) * each]:
            found = found + arrived[0].astype(jnp.float32)
        total[:, head * cols : (head + 1) * cols] = found
    for bits, out in enumerate(outs):
        out[...] = total[at_offset(at_ref[0] ^ bits, size)]


def finish(at, parts, waits):
    _, chunk, cols = parts[0][0].shape
    heads = len(parts)
    piece = jax.ShapeDtypeStruct((chunk // LANES, heads * cols), jnp.float32)
    return small_call(
        functools.partial(finish_kernel, heads=heads, each=len(parts[0])),
        "finish", at, [value for part in parts for value in part], [piece] * LANES,
        [pltpu.VMEM((chunk, heads * cols), jnp.float32)],
        waits=waits,
    )


def passed_round(pieces):
    return [exchanged(piece, bits) if bits else piece for bits, piece in enumerate(pieces)]


def local(features, queries, kv_weight, upstream):
    tokens = features[0]
    size = tokens.shape[0]
    weight_rows, kv_width = kv_weight.shape
    width = kv_width // 2
    lane_width = width // LANES
    heads = lane_width // HEAD_DIM
    rows = lax.axis_size("seq") // LANES
    place = lax.axis_index("seq")
    lane = place % LANES
    row = place // LANES
    half = lax.axis_index("dp")
    core = place % 2

    here = jnp.stack([lane, half, core]).astype(jnp.int32)
    pair_pieces, lane_weight = deal(here, queries, upstream, kv_weight)
    other_lane_weight = swapped(lane_weight)
    across = exchanged(tokens, 2)
    beside = exchanged(tokens, 1)
    diagonal = exchanged(across, 1)
    row_tokens = (tokens, beside, across, diagonal)

    owns = project(here, row_tokens, (lane_weight, other_lane_weight))
    windows = [(own, shifted(own, 1)) for own in owns]

    part = take_rows(here, kv_weight)
    own_pairs, (part,) = place_rows(here, passed_round(pair_pieces), owns[:1], (part,))
    next_pairs = [shifted(own_pair, -1) for own_pair in own_pairs]

    fetched = swapped(part)

    at = jnp.stack([row, lane]).astype(jnp.int32)
    shared, turns = [], []
    for head in range(heads):
        turns.append(turned_over(at, windows[head][1]))
        own_stats, next_stats = softmax_stats(
            at, own_pairs[head], next_pairs[head], windows[head], size, (turns[-1],)
        )
        shared.append(
            (own_stats, turned_round(next_stats, 1), next_stats, turned_round(own_stats, -1))
        )
    gained, next_out = [], ()
    for head in range(heads):
        gained.append(
            attention_grads(
                at, own_pairs[head], next_pairs[head], (*windows[head], turns[head]),
                shared[head], next_out, size,
                (shared[-1][0],),
            )
        )
        next_out = (gained[-1][1],)
    own_outs = [found[0] for found in gained]

    bits = jnp.stack([(row >> index) % 2 for index in range(rows.bit_length() - 1)])
    kv_pieces, parts = [], []
    waits, through = (gained[-1][3],), (fetched,)
    arrived_out = shifted(next_out[0], 1)
    for head, (_, _, near_grad, own_grad) in enumerate(gained):
        kv_pieces, kept, sent, handed = spread(
            here, row_tokens, own_grad, shifted(near_grad, -1), kv_pieces, rows, waits, through
        )
        if through:
            (fetched,) = handed
            passed = exchanged(fetched, 1)
        if head == heads - 1:
            kv_found = go_round(here, kv_pieces)
            out_found = go_round(here, settle_outs(here, own_outs, arrived_out, (sent,)))
        waits, through = (), ()
        arrived = [swapped(sent)]
        distance = 1
        while distance < rows:
            last = head == heads - 1 and 2 * distance == rows
            kept, sent = merge(
                bits, distance.bit_length() - 1, kept, arrived, kv_found[2:] if last else ()
            )
            arrived = [moved(sent, distance * LANES, 0)]
            if not waits:
                waits = (sent,)
            distance *= 2
        parts.append((kept, *arrived))

    feature_grad, feature_token = feature_grads(
        here,
        kv_found,
        (kv_weight, fetched, passed),
        (sent,),
    )
    attended, query_grad, token = place_heads(here, out_found)
    pieces = passed_round(finish(here, parts, (feature_token,)))
    weight_grad = place_weight(here, pieces, (token,))
    return (attended, query_grad, feature_grad, weight_grad)


def solution(mesh):
    return jax.shard_map(
        local,
        mesh=mesh,
        in_specs=(P("dp", "seq", None), P("dp", "seq", None), P("dp", None), P("dp", "seq", None)),
        out_specs=(
            P("dp", "seq", None),
            P("dp", "seq", None),
            P("dp", "seq", None),
            P(("dp", "seq"), None),
        ),
        check_vma=False,
    )
```
